32 devices in a mesh: dp: 4 (over y, x), seq: 8 (over z, core).
Axes of the slice: x: 2, y: 2, z: 4, core: 2. Of those that a mesh axis runs over, the one named last changes fastest.
Arguments:
- queries: bfloat16 [4, 1024, 4096], P('dp', 'seq'), may hold values from -6 to 6
- key_states: bfloat16 [4, 1024, 1024], P('dp', 'seq'), may hold values from -8 to 8
- value_states: bfloat16 [4, 1024, 1024], P('dp', 'seq'), may hold values from -6 to 6
- sink_logit: float32 [32], P('seq'), may hold values from 7 to 12
- out_grad: bfloat16 [4, 1024, 4096], P('dp', 'seq'), may hold values from -16 to 16
- block_table: int32 [32, 8, 8], P('seq'), may hold values from 0 to 7, as said below
Outputs:
- query_grad: bfloat16 [4, 1024, 4096], P('dp', 'seq')
- key_grad: bfloat16 [4, 1024, 1024], P('dp', 'seq')
- value_grad: bfloat16 [4, 1024, 1024], P('dp', 'seq')
- sink_grad: float32 [32], P('seq')
The draws below stay inside these ranges and needn't reach their ends.
Inputs may be any that keep to these rules, and one draw needn't show every extreme that they name: `block_table`: each row lists 8 different key blocks; among them are the query's own block, the two blocks beside it (cyclically) and block 0.
All inputs are finite; a program needn't handle non-finite values.
Results may differ from the reference program's by a relative error of at most 0.0066.
Values may be sent and summed in bfloat16 or wider, within the bound.
A program may use at most 64 MiB of HBM per device.

```python
import jax
import jax.numpy as jnp
from jax import lax

HEADS = 32
KV_HEADS = 8
HEAD_DIM = 128
BLOCK = 128
KB = 8
SEQS = 4
LEN = 1024
NB = 8


def draw_queries(key, part):
    shape = (SEQS, LEN, HEADS * HEAD_DIM)
    values = jnp.clip(jax.random.normal(jax.random.fold_in(key, 1), shape, jnp.float32), -6.0, 6.0)
    return values.astype(jnp.bfloat16)


def draw_key_states(key, part):
    shape = (SEQS, LEN, KV_HEADS * HEAD_DIM)
    values = jnp.clip(2.5 * jax.random.normal(jax.random.fold_in(key, 2), shape, jnp.float32), -8.0, 8.0)
    return values.astype(jnp.bfloat16)


def draw_out_grad(key, part):
    shape = (SEQS, LEN, HEADS * HEAD_DIM)
    sequence = lax.broadcasted_iota(jnp.int32, (SEQS, 1, 1), 0).astype(jnp.float32)
    factor = 1.0 + 2.0 * sequence / max(SEQS - 1, 1)
    values = jnp.clip(jax.random.normal(jax.random.fold_in(key, 3), shape, jnp.float32), -4.0, 4.0)
    return (values * factor).astype(jnp.bfloat16)


def draw_block_table(key, part):
    rows = lax.broadcasted_iota(jnp.int32, (HEADS, NB, NB), 1)
    columns = lax.broadcasted_iota(jnp.int32, (HEADS, NB, NB), 2)
    noise = jax.random.randint(jax.random.fold_in(key, 4), (HEADS, NB, NB), 0, 2 ** 20, jnp.int32)
    needed = (columns == rows) | (columns == (rows + 1) % NB) | (columns == (rows + NB - 1) % NB) | (columns == 0)
    ranking = noise * NB + columns + jnp.where(needed, 2 ** 30, 0).astype(jnp.int32)
    chosen = lax.top_k(ranking, KB)[1]
    return chosen.astype(jnp.int32)


def levels(stream_key, shape, pieces, low, top_value):
    def one(position, blocks):
        steps = jax.random.uniform(jax.random.fold_in(jax.random.fold_in(stream_key, 6), position), (blocks,), jnp.float32, low / len(pieces), top_value / len(pieces))
        return jnp.repeat(jnp.exp(steps), shape[position] // blocks).reshape((-1,) + (1,) * (len(shape) - position - 1))

    gain = one(*pieces[0])
    for cut in pieces[1:]:
        gain = gain * one(*cut)
    return gain


def gaussian(rng, shape, width, most, split=(), kind=jnp.bfloat16):
    drawn = jax.random.normal(rng, shape, jnp.float32) * width
    if len(split) > 0:
        drawn = levels(rng, shape, split, -0.22, 0.18) * drawn
    return jnp.clip(drawn, min=-most, max=most).astype(kind)


def setup_inputs(seed: int = 0) -> dict:
    key_of = jax.random.split(jax.random.key(seed), 7)
    return {
        "queries": draw_queries(jax.random.fold_in(key_of[6], 71), 0),
        "key_states": draw_key_states(jax.random.fold_in(key_of[6], 71), 0),
        "value_states": gaussian(key_of[2], (SEQS, LEN, KV_HEADS * HEAD_DIM), 1.0, 6.0, ((0, 4), (1, 8))),
        "sink_logit": jnp.clip(7.0 + 5.0 * jax.random.uniform(key_of[3], (HEADS,), jnp.float32) ** levels(key_of[3], (HEADS,), ((0, 8),), -0.2, 0.2), 7.0, 12.0),
        "out_grad": draw_out_grad(jax.random.fold_in(key_of[6], 71), 0),
        "block_table": draw_block_table(jax.random.fold_in(key_of[6], 71), 0),
    }


def head_block(query_head, key_head, value_head, grad_head, sink_value, table):
    scale = HEAD_DIM ** -0.5
    query_blocks = query_head.reshape(NB, BLOCK, HEAD_DIM).astype(jnp.float32)
    key_pick = key_head.reshape(NB, BLOCK, HEAD_DIM)[table].reshape(NB, KB * BLOCK, HEAD_DIM).astype(jnp.float32)
    value_pick = value_head.reshape(NB, BLOCK, HEAD_DIM)[table].reshape(NB, KB * BLOCK, HEAD_DIM).astype(jnp.float32)
    grad_blocks = grad_head.reshape(NB, BLOCK, HEAD_DIM).astype(jnp.float32)
    scores = jnp.einsum('nqd,nkd->nqk', query_blocks, key_pick) * scale
    top = jnp.maximum(jnp.max(scores, -1), sink_value)
    weights = jnp.exp(scores - top[..., None])
    sink_weight = jnp.exp(sink_value - top)
    total = jnp.sum(weights, -1) + sink_weight
    probs = weights / total[..., None]
    sink_prob = sink_weight / total
    probs_low = probs.astype(jnp.bfloat16).astype(jnp.float32)
    attended = jnp.einsum('nqk,nkd->nqd', probs_low, value_pick)
    delta = jnp.sum(grad_blocks * attended, -1)
    dprobs = jnp.einsum('nqd,nkd->nqk', grad_blocks, value_pick)
    dscores = (probs * (dprobs - delta[..., None])).astype(jnp.bfloat16).astype(jnp.float32)
    query_grad = jnp.einsum('nqk,nkd->nqd', dscores, key_pick) * scale
    key_terms = jnp.einsum('nqk,nqd->nkd', dscores, query_blocks) * scale
    value_terms = jnp.einsum('nqk,nqd->nkd', probs_low, grad_blocks)
    flat_table = table.reshape(-1)
    key_grad = jnp.zeros((NB, BLOCK, HEAD_DIM), jnp.float32).at[flat_table].add(key_terms.reshape(NB * KB, BLOCK, HEAD_DIM))
    value_grad = jnp.zeros((NB, BLOCK, HEAD_DIM), jnp.float32).at[flat_table].add(value_terms.reshape(NB * KB, BLOCK, HEAD_DIM))
    sink_grad = -jnp.sum(sink_prob * delta)
    return query_grad.reshape(LEN, HEAD_DIM), key_grad.reshape(LEN, HEAD_DIM), value_grad.reshape(LEN, HEAD_DIM), sink_grad


def reference(queries, key_states, value_states, sink_logit, out_grad, block_table):
    group = HEADS // KV_HEADS

    def per_sequence(items):
        query_seq, key_seq, value_seq, grad_seq = items
        query_heads = query_seq.reshape(LEN, HEADS, HEAD_DIM).transpose(1, 0, 2)
        grad_heads = grad_seq.reshape(LEN, HEADS, HEAD_DIM).transpose(1, 0, 2)
        key_heads = key_seq.reshape(LEN, KV_HEADS, HEAD_DIM).transpose(1, 0, 2)
        value_heads = value_seq.reshape(LEN, KV_HEADS, HEAD_DIM).transpose(1, 0, 2)

        def per_head(head_items):
            query_head, grad_head, sink_value, table, head_index = head_items
            shared = head_index // group
            key_head = lax.dynamic_index_in_dim(key_heads, shared, 0, keepdims=False)
            value_head = lax.dynamic_index_in_dim(value_heads, shared, 0, keepdims=False)
            return head_block(query_head, key_head, value_head, grad_head, sink_value, table)

        query_grads, key_grads, value_grads, sink_grads = lax.map(
            per_head, (query_heads, grad_heads, sink_logit, block_table, jnp.arange(HEADS, dtype=jnp.int32)))
        key_sum = key_grads.reshape(KV_HEADS, group, LEN, HEAD_DIM).sum(1)
        value_sum = value_grads.reshape(KV_HEADS, group, LEN, HEAD_DIM).sum(1)
        return (query_grads.transpose(1, 0, 2).reshape(LEN, HEADS * HEAD_DIM).astype(jnp.bfloat16),
                key_sum.transpose(1, 0, 2).reshape(LEN, KV_HEADS * HEAD_DIM).astype(jnp.bfloat16),
                value_sum.transpose(1, 0, 2).reshape(LEN, KV_HEADS * HEAD_DIM).astype(jnp.bfloat16),
                sink_grads)

    results = lax.map(per_sequence, (queries, key_states, value_states, out_grad))
    return (results[0], results[1], results[2], jnp.sum(results[3], 0))
```

```python
import jax
import jax.numpy as jnp
from jax import lax
from jax.experimental import pallas as pl
from jax.experimental.pallas import tpu as pltpu
from jax.sharding import PartitionSpec as P

HEADS = 32
KV_HEADS = 8
HEAD_DIM = 128
BLOCK = 128
KB = 8


def sparse_shards(queries, key_states, value_states, sink_logit, out_grad, block_table):
    devices = lax.axis_size("seq")
    tokens_here = queries.shape[1]
    length = tokens_here * devices
    heads_here = HEADS // devices
    group = HEADS // KV_HEADS
    repeats = devices // KV_HEADS
    blocks = length // BLOCK
    scale = HEAD_DIM ** (-0.5)
    key_wide = jnp.repeat(key_states.reshape(1, tokens_here, KV_HEADS, 1, HEAD_DIM), group, axis=3)
    key_wide = key_wide.reshape(1, tokens_here, HEADS * HEAD_DIM)
    value_wide = jnp.repeat(
        value_states.reshape(1, tokens_here, KV_HEADS, 1, HEAD_DIM), group, axis=3
    )
    value_wide = value_wide.reshape(1, tokens_here, HEADS * HEAD_DIM)
    query_all, grad_all, key_all, value_all = (
        lax.all_to_all(queries, "seq", split_axis=2, concat_axis=1, tiled=True),
        lax.all_to_all(out_grad, "seq", split_axis=2, concat_axis=1, tiled=True),
        lax.all_to_all(key_wide, "seq", split_axis=2, concat_axis=1, tiled=True),
        lax.all_to_all(value_wide, "seq", split_axis=2, concat_axis=1, tiled=True),
    )
    key_rows = key_all[0, :, :HEAD_DIM]
    value_rows = value_all[0, :, :HEAD_DIM]
    group_blocks = max(4, blocks // 8)
    step_count = blocks // group_blocks
    query_steps = query_all.reshape(step_count, group_blocks, BLOCK, heads_here, HEAD_DIM)
    grad_steps = grad_all.reshape(step_count, group_blocks, BLOCK, heads_here, HEAD_DIM)
    table_steps = block_table.reshape(heads_here, step_count, group_blocks, KB).transpose(
        1, 0, 2, 3
    )
    key_table = key_rows.reshape(blocks, BLOCK, HEAD_DIM)
    value_table = value_rows.reshape(blocks, BLOCK, HEAD_DIM)
    sink_column = sink_logit[:, None, None]

    def advance(carry, items):
        key_acc, value_acc, sink_acc = carry
        query_group, grad_group, table_group = items
        key_pick = key_table[table_group].reshape(heads_here, group_blocks, KB * BLOCK, HEAD_DIM)
        value_pick = value_table[table_group].reshape(
            heads_here, group_blocks, KB * BLOCK, HEAD_DIM
        )
        scores = (
            jnp.einsum("gqhd,hgkd->hgqk", query_group, key_pick, preferred_element_type=jnp.float32)
            * scale
        )
        top = jnp.maximum(jnp.max(scores, -1), sink_column)
        weights = jnp.exp(scores - top[..., None])
        sink_weight = jnp.exp(sink_column - top)
        total = jnp.sum(weights, -1) + sink_weight
        probs = weights / total[..., None]
        sink_prob = sink_weight / total
        probs_low = probs.astype(jnp.bfloat16)
        attended = jnp.einsum(
            "hgqk,hgkd->gqhd", probs_low, value_pick, preferred_element_type=jnp.float32
        )
        delta_rows = jnp.sum(grad_group.astype(jnp.float32) * attended, -1)
        delta = jnp.transpose(delta_rows, (2, 0, 1))
        dprobs = jnp.einsum(
            "gqhd,hgkd->hgqk", grad_group, value_pick, preferred_element_type=jnp.float32
        )
        dscores = (probs * (dprobs - delta[..., None])).astype(jnp.bfloat16)
        query_part = (
            jnp.einsum("hgqk,hgkd->gqhd", dscores, key_pick, preferred_element_type=jnp.float32)
            * scale
        ).astype(jnp.bfloat16)
        key_terms = (
            jnp.einsum("hgqk,gqhd->hgkd", dscores, query_group, preferred_element_type=jnp.float32)
            * scale
        )
        value_terms = jnp.einsum(
            "hgqk,gqhd->hgkd", probs_low, grad_group, preferred_element_type=jnp.float32
        )
        flat_table = table_group.reshape(-1)
        key_acc = key_acc.at[flat_table].add(
            key_terms.reshape(heads_here * group_blocks * KB, BLOCK, HEAD_DIM)
        )
        value_acc = value_acc.at[flat_table].add(
            value_terms.reshape(heads_here * group_blocks * KB, BLOCK, HEAD_DIM)
        )
        sink_acc = sink_acc - jnp.sum(sink_prob * delta, axis=(1, 2))
        return ((key_acc, value_acc, sink_acc), query_part)

    start = (
        jnp.zeros((blocks, BLOCK, HEAD_DIM), jnp.float32),
        jnp.zeros((blocks, BLOCK, HEAD_DIM), jnp.float32),
        jnp.zeros((heads_here,), jnp.float32),
    )
    finished, query_parts = lax.scan(advance, start, (query_steps, grad_steps, table_steps))
    key_acc, value_acc, sink_acc = finished
    query_local = query_parts.reshape(1, length, heads_here * HEAD_DIM)
    query_grad = lax.all_to_all(query_local, "seq", split_axis=1, concat_axis=2, tiled=True)
    kv_terms = jnp.stack(
        [key_acc.reshape(length, HEAD_DIM), value_acc.reshape(length, HEAD_DIM)], 0
    )
    returned = lax.all_to_all(kv_terms, "seq", split_axis=1, concat_axis=2, tiled=True)
    kv_back = returned.reshape(2, tokens_here, KV_HEADS, repeats, HEAD_DIM).sum(3)
    kv_back = kv_back.reshape(2, tokens_here, KV_HEADS * HEAD_DIM)
    key_grad = kv_back[0:1].astype(jnp.bfloat16)
    value_grad = kv_back[1:2].astype(jnp.bfloat16)
    sink_grad = lax.psum(sink_acc, "dp")
    return (query_grad, key_grad, value_grad, sink_grad)


F32 = jnp.float32
BF16 = jnp.bfloat16
GROUP = HEADS // KV_HEADS
SCALE = HEAD_DIM ** (-0.5)


def group_terms(keys, values, queries, grads, sink_row):
    nt = (((1,), (1,)), ((), ()))
    tn = (((0,), (0,)), ((), ()))
    scores = lax.dot_general(keys, queries, nt, preferred_element_type=F32) * SCALE
    dprobs = lax.dot_general(values, grads, nt, preferred_element_type=F32)
    top = jnp.maximum(jnp.max(scores, 0, keepdims=True), sink_row)
    weights = jnp.exp(scores - top)
    sink_weight = jnp.exp(sink_row - top)
    inverse = 1.0 / (jnp.sum(weights, 0, keepdims=True) + sink_weight)
    probs = weights * inverse
    probs_low = probs.astype(BF16)
    delta = jnp.sum(probs_low.astype(F32) * dprobs, 0, keepdims=True)
    dscores = (probs * (dprobs - delta)).astype(BF16)
    value_terms = jnp.dot(probs_low, grads, preferred_element_type=F32)
    key_terms = jnp.dot(dscores, queries, preferred_element_type=F32)
    query_terms = lax.dot_general(keys, dscores, tn, preferred_element_type=F32)
    return key_terms, value_terms, query_terms.T * SCALE, -(sink_weight * inverse) * delta


def dense_kernel(q_ref, g_ref, k_ref, v_ref, sink_ref, dq_ref, dk_ref, dv_ref, ds_ref):
    keys, values = k_ref[...], v_ref[...]
    key_sum = value_sum = None
    for half in range(2):
        heads = range(half * GROUP // 2, (half + 1) * GROUP // 2)
        cuts = [slice(j * HEAD_DIM, (j + 1) * HEAD_DIM) for j in heads]
        queries = jnp.concatenate([q_ref[:, cut] for cut in cuts], 0)
        grads = jnp.concatenate([g_ref[:, cut] for cut in cuts], 0)
        rows = queries.shape[0]
        span = slice(half * rows, (half + 1) * rows)
        key_terms, value_terms, query_terms, sink_terms = group_terms(
            keys, values, queries, grads, sink_ref[0, :, span]
        )
        key_sum = key_terms if key_sum is None else key_sum + key_terms
        value_sum = value_terms if value_sum is None else value_sum + value_terms
        for i, cut in enumerate(cuts):
            part = query_terms[i * rows // 2 : (i + 1) * rows // 2]
            dq_ref[:, cut] = part.astype(BF16)
        ds_ref[0, :, span] = sink_terms
    dk_ref[...] = (key_sum * SCALE).astype(BF16)
    dv_ref[...] = value_sum.astype(BF16)


def dense_shards(queries, key_states, value_states, sink_logit, out_grad, block_table):
    devices = lax.axis_size("seq")
    here = queries.shape[1]
    length = here * devices
    wide = GROUP * HEAD_DIM
    key_all = lax.all_gather(key_states[0], "seq", axis=0, tiled=True)
    value_all = lax.all_gather(value_states[0], "seq", axis=0, tiled=True)
    sink_all = lax.all_gather(sink_logit, "seq", axis=0, tiled=True)
    sink_rows = jnp.repeat(sink_all.reshape(KV_HEADS, GROUP), here, axis=1)[:, None, :]
    rows = pl.BlockSpec((here, wide), lambda h: (0, h))
    cols = pl.BlockSpec((length, HEAD_DIM), lambda h: (0, h))
    line = pl.BlockSpec((1, 1, GROUP * here), lambda h: (h, 0, 0))
    flat = KV_HEADS * HEAD_DIM
    query_grad, key_part, value_part, sink_part = pl.pallas_call(
        dense_kernel,
        grid=(KV_HEADS,),
        in_specs=[rows, rows, cols, cols, line],
        out_specs=[rows, cols, cols, line],
        out_shape=[
            jax.ShapeDtypeStruct((here, HEADS * HEAD_DIM), BF16),
            jax.ShapeDtypeStruct((length, flat), BF16),
            jax.ShapeDtypeStruct((length, flat), BF16),
            jax.ShapeDtypeStruct((KV_HEADS, 1, GROUP * here), F32),
        ],
        compiler_params=pltpu.CompilerParams(vmem_limit_bytes=48 * 2**20),
    )(queries[0], out_grad[0], key_all, value_all, sink_rows)
    key_grad = lax.psum_scatter(key_part, "seq", scatter_dimension=0, tiled=True)
    value_grad = lax.psum_scatter(value_part, "seq", scatter_dimension=0, tiled=True)
    sink_sum = lax.psum(sink_part.reshape(HEADS, here).sum(1), ("dp", "seq"))
    mine = HEADS // devices
    sink_grad = lax.dynamic_slice_in_dim(sink_sum, lax.axis_index("seq") * mine, mine)
    return query_grad[None], key_grad[None], value_grad[None], sink_grad


def shards(queries, key_states, value_states, sink_logit, out_grad, block_table):
    blocks = queries.shape[1] * lax.axis_size("seq") // BLOCK
    part = dense_shards if blocks == KB else sparse_shards
    return part(queries, key_states, value_states, sink_logit, out_grad, block_table)


def solution(mesh):
    in_specs = (
        P("dp", "seq", None),
        P("dp", "seq", None),
        P("dp", "seq", None),
        P("seq"),
        P("dp", "seq", None),
        P("seq", None, None),
    )
    out_specs = (P("dp", "seq", None), P("dp", "seq", None), P("dp", "seq", None), P("seq"))
    return jax.shard_map(shards, mesh=mesh, in_specs=in_specs, out_specs=out_specs, check_vma=False)
```

```python
import jax
import jax.numpy as jnp
from jax import lax
from jax.experimental import pallas as pl
from jax.experimental.pallas import tpu as pltpu
from jax.sharding import PartitionSpec as P

HEADS = 32
KV_HEADS = 8
HEAD_DIM = 128
BLOCK = 128
KB = 8


def sparse_shards(queries, key_states, value_states, sink_logit, out_grad, block_table):
    devices = lax.axis_size("seq")
    tokens_here = queries.shape[1]
    length = tokens_here * devices
    heads_here = HEADS // devices
    group = HEADS // KV_HEADS
    repeats = devices // KV_HEADS
    blocks = length // BLOCK
    scale = HEAD_DIM ** (-0.5)
    key_wide = jnp.repeat(key_states.reshape(1, tokens_here, KV_HEADS, 1, HEAD_DIM), group, axis=3)
    key_wide = key_wide.reshape(1, tokens_here, HEADS * HEAD_DIM)
    value_wide = jnp.repeat(
        value_states.reshape(1, tokens_here, KV_HEADS, 1, HEAD_DIM), group, axis=3
    )
    value_wide = value_wide.reshape(1, tokens_here, HEADS * HEAD_DIM)
    query_all, grad_all, key_all, value_all = (
        lax.all_to_all(queries, "seq", split_axis=2, concat_axis=1, tiled=True),
        lax.all_to_all(out_grad, "seq", split_axis=2, concat_axis=1, tiled=True),
        lax.all_to_all(key_wide, "seq", split_axis=2, concat_axis=1, tiled=True),
        lax.all_to_all(value_wide, "seq", split_axis=2, concat_axis=1, tiled=True),
    )
    key_rows = key_all[0, :, :HEAD_DIM]
    value_rows = value_all[0, :, :HEAD_DIM]
    group_blocks = max(4, blocks // 8)
    step_count = blocks // group_blocks
    query_steps = query_all.reshape(step_count, group_blocks, BLOCK, heads_here, HEAD_DIM)
    grad_steps = grad_all.reshape(step_count, group_blocks, BLOCK, heads_here, HEAD_DIM)
    table_steps = block_table.reshape(heads_here, step_count, group_blocks, KB).transpose(
        1, 0, 2, 3
    )
    key_table = key_rows.reshape(blocks, BLOCK, HEAD_DIM)
    value_table = value_rows.reshape(blocks, BLOCK, HEAD_DIM)
    sink_column = sink_logit[:, None, None]

    def advance(carry, items):
        key_acc, value_acc, sink_acc = carry
        query_group, grad_group, table_group = items
        key_pick = key_table[table_group].reshape(heads_here, group_blocks, KB * BLOCK, HEAD_DIM)
        value_pick = value_table[table_group].reshape(
            heads_here, group_blocks, KB * BLOCK, HEAD_DIM
        )
        scores = (
            jnp.einsum("gqhd,hgkd->hgqk", query_group, key_pick, preferred_element_type=jnp.float32)
            * scale
        )
        top = jnp.maximum(jnp.max(scores, -1), sink_column)
        weights = jnp.exp(scores - top[..., None])
        sink_weight = jnp.exp(sink_column - top)
        total = jnp.sum(weights, -1) + sink_weight
        probs = weights / total[..., None]
        sink_prob = sink_weight / total
        probs_low = probs.astype(jnp.bfloat16)
        attended = jnp.einsum(
            "hgqk,hgkd->gqhd", probs_low, value_pick, preferred_element_type=jnp.float32
        )
        delta_rows = jnp.sum(grad_group.astype(jnp.float32) * attended, -1)
        delta = jnp.transpose(delta_rows, (2, 0, 1))
        dprobs = jnp.einsum(
            "gqhd,hgkd->hgqk", grad_group, value_pick, preferred_element_type=jnp.float32
        )
        dscores = (probs * (dprobs - delta[..., None])).astype(jnp.bfloat16)
        query_part = (
            jnp.einsum("hgqk,hgkd->gqhd", dscores, key_pick, preferred_element_type=jnp.float32)
            * scale
        ).astype(jnp.bfloat16)
        key_terms = (
            jnp.einsum("hgqk,gqhd->hgkd", dscores, query_group, preferred_element_type=jnp.float32)
            * scale
        )
        value_terms = jnp.einsum(
            "hgqk,gqhd->hgkd", probs_low, grad_group, preferred_element_type=jnp.float32
        )
        flat_table = table_group.reshape(-1)
        key_acc = key_acc.at[flat_table].add(
            key_terms.reshape(heads_here * group_blocks * KB, BLOCK, HEAD_DIM)
        )
        value_acc = value_acc.at[flat_table].add(
            value_terms.reshape(heads_here * group_blocks * KB, BLOCK, HEAD_DIM)
        )
        sink_acc = sink_acc - jnp.sum(sink_prob * delta, axis=(1, 2))
        return ((key_acc, value_acc, sink_acc), query_part)

    start = (
        jnp.zeros((blocks, BLOCK, HEAD_DIM), jnp.float32),
        jnp.zeros((blocks, BLOCK, HEAD_DIM), jnp.float32),
        jnp.zeros((heads_here,), jnp.float32),
    )
    finished, query_parts = lax.scan(advance, start, (query_steps, grad_steps, table_steps))
    key_acc, value_acc, sink_acc = finished
    query_local = query_parts.reshape(1, length, heads_here * HEAD_DIM)
    query_grad = lax.all_to_all(query_local, "seq", split_axis=1, concat_axis=2, tiled=True)
    kv_terms = jnp.stack(
        [key_acc.reshape(length, HEAD_DIM), value_acc.reshape(length, HEAD_DIM)], 0
    )
    returned = lax.all_to_all(kv_terms, "seq", split_axis=1, concat_axis=2, tiled=True)
    kv_back = returned.reshape(2, tokens_here, KV_HEADS, repeats, HEAD_DIM).sum(3)
    kv_back = kv_back.reshape(2, tokens_here, KV_HEADS * HEAD_DIM)
    key_grad = kv_back[0:1].astype(jnp.bfloat16)
    value_grad = kv_back[1:2].astype(jnp.bfloat16)
    sink_grad = lax.psum(sink_acc, "dp")
    return (query_grad, key_grad, value_grad, sink_grad)


F32 = jnp.float32
BF16 = jnp.bfloat16
GROUP = HEADS // KV_HEADS
SCALE = HEAD_DIM ** (-0.5)


def group_terms(keys, values, queries, grads, sink_row):
    nt = (((1,), (1,)), ((), ()))
    tn = (((0,), (0,)), ((), ()))
    scores = lax.dot_general(keys, queries, nt, preferred_element_type=F32) * SCALE
    dprobs = lax.dot_general(values, grads, nt, preferred_element_type=F32)
    top = jnp.maximum(jnp.max(scores, 0, keepdims=True), sink_row)
    weights = jnp.exp(scores - top)
    sink_weight = jnp.exp(sink_row - top)
    inverse = 1.0 / (jnp.sum(weights, 0, keepdims=True) + sink_weight)
    probs = weights * inverse
    probs_low = probs.astype(BF16)
    delta = jnp.sum(probs_low.astype(F32) * dprobs, 0, keepdims=True)
    dscores = (probs * (dprobs - delta)).astype(BF16)
    value_terms = jnp.dot(probs_low, grads, preferred_element_type=F32)
    key_terms = jnp.dot(dscores, queries, preferred_element_type=F32)
    query_terms = lax.dot_general(keys, dscores, tn, preferred_element_type=F32)
    return key_terms, value_terms, query_terms.T * SCALE, -(sink_weight * inverse) * delta


def dense_kernel(
    q_ref, g_ref, k_ref, v_ref, sink_ref,
    dq_ref, dk_ref, dv_ref, ds_ref,
    kv_all, acc, part, pair_out, pair_in, right_out, right_in, left_out, left_in,
    sink_all, sink_part, sink_in, sink_dp,
    right_s, right_r, left_s, left_r, sib_s, sib_r, pair_s, pair_r,
    sumr_s, sumr_r, suml_s, suml_r, logit_s, logit_r, sg_s, sg_r, dp_s, dp_r,
):
    devices = lax.axis_size("seq")
    chips = devices // 2
    last = chips - 1
    dps = lax.axis_size("dp")
    me = lax.axis_index("seq")
    my_dp = lax.axis_index("dp")
    chip = lax.div(me, 2)
    lane = lax.rem(me, 2)
    sibling = me + 1 - 2 * lane
    here = HEAD_DIM
    wide = GROUP * HEAD_DIM

    def remote(src, dst, send_sem, recv_sem, **target):
        return pltpu.make_async_remote_copy(
            src_ref=src, dst_ref=dst, send_sem=send_sem, recv_sem=recv_sem,
            device_id=target, device_id_type=pl.DeviceIdType.MESH,
        )

    def shard(h, z, which):
        return kv_all.at[:, h, 2 * z + which]

    def go_right(h, k, z):
        ref = shard(h, z, lane)
        return remote(ref, ref, right_s.at[h, k], right_r.at[h, k], seq=me + 2)

    def go_left(h, k, z):
        ref = shard(h, z, lane)
        return remote(ref, ref, left_s.at[h, k], left_r.at[h, k], seq=me - 2)

    def go_across(h, z, which):
        ref = shard(h, z, which)
        return remote(ref, ref, sib_s.at[h, z], sib_r.at[h, z], seq=sibling)

    def go_pair(h):
        return remote(pair_out.at[h], pair_in.at[h], pair_s.at[h], pair_r.at[h], seq=sibling)

    def sum_right(h, d):
        return remote(
            right_out.at[h, d], right_in.at[h, d], sumr_s.at[h, d], sumr_r.at[h, d], seq=me + 2
        )

    def sum_left(h, d):
        return remote(
            left_out.at[h, d], left_in.at[h, d], suml_s.at[h, d], suml_r.at[h, d], seq=me - 2
        )

    def logit(i, owner):
        ref = sink_all.at[owner]
        return remote(ref, ref, logit_s.at[i], logit_r.at[i], seq=lax.rem(me + i, devices))

    def sink_send(h):
        return remote(sink_part.at[h], sink_in.at[me], sg_s.at[h], sg_r.at[me], seq=h)

    def sink_recv(p):
        return remote(sink_part.at[p], sink_in.at[p], sg_s.at[p], sg_r.at[p], seq=p)

    def across_dp(i, owner):
        ref = sink_dp.at[owner]
        return remote(ref, ref, dp_s.at[i], dp_r.at[i], dp=lax.rem(my_dp + i, dps))

    barrier = pltpu.get_barrier_semaphore()
    for i in range(1, devices):
        pl.semaphore_signal(
            barrier, inc=1, device_id={"seq": lax.rem(me + i, devices)},
            device_id_type=pl.DeviceIdType.MESH,
        )
    for i in range(1, dps):
        pl.semaphore_signal(
            barrier, inc=1, device_id={"dp": lax.rem(my_dp + i, dps)},
            device_id_type=pl.DeviceIdType.MESH,
        )

    for h in range(KV_HEADS):
        cut = slice(h * HEAD_DIM, (h + 1) * HEAD_DIM)
        kv_all[0, h, me] = k_ref[:, cut]
        kv_all[1, h, me] = v_ref[:, cut]
    sink_all[me] = sink_ref[...]
    sink_part[...] = jnp.zeros_like(sink_part)
    pl.semaphore_wait(barrier, devices - 1 + dps - 1)

    def send_own(h):
        @pl.when(chip < last)
        def _():
            go_right(h, 0, chip).start()

        @pl.when(chip > 0)
        def _():
            go_left(h, 0, chip).start()

        go_across(h, chip, lane).start()

    send_own(0)
    for i in range(1, devices):
        logit(i, me).start()
    send_own(1)
    for i in range(1, devices):
        logit(i, lax.rem(me - i + devices, devices)).wait_recv()

    def hand_on(h, k):
        @pl.when(chip >= k)
        def _():
            go_right(h, k - 1, chip - k).wait_recv()
            if k < last:

                @pl.when(chip < last)
                def _():
                    go_right(h, k, chip - k).start()

            go_across(h, chip - k, lane).start()

        @pl.when(chip + k <= last)
        def _():
            go_left(h, k - 1, chip + k).wait_recv()
            if k < last:

                @pl.when(chip > 0)
                def _():
                    go_left(h, k, chip + k).start()

            go_across(h, chip + k, lane).start()

    def compute(h):
        for z in range(chips):
            go_across(h, z, 1 - lane).wait_recv()
        keys = kv_all[0, h].reshape(devices * here, HEAD_DIM)
        values = kv_all[1, h].reshape(devices * here, HEAD_DIM)
        key_sum = value_sum = None
        for half in range(2):
            heads = range(half * GROUP // 2, (half + 1) * GROUP // 2)
            cuts = [
                pl.ds(pl.multiple_of(h * wide + j * HEAD_DIM, HEAD_DIM), HEAD_DIM) for j in heads
            ]
            queries = jnp.concatenate([q_ref[:, cut] for cut in cuts], 0)
            grads = jnp.concatenate([g_ref[:, cut] for cut in cuts], 0)
            sink_row = jnp.concatenate([sink_all[h, j : j + 1, :] for j in heads], 1)
            key_terms, value_terms, query_terms, sink_terms = group_terms(
                keys, values, queries, grads, sink_row
            )
            key_sum = key_terms if key_sum is None else key_sum + key_terms
            value_sum = value_terms if value_sum is None else value_sum + value_terms
            for i, j in enumerate(heads):
                span = slice(i * here, (i + 1) * here)
                dq_ref[:, cuts[i]] = query_terms[span].astype(BF16)
                sink_part[h, j : j + 1, :] = sink_terms[:, span]
        acc[0] = (key_sum * SCALE).reshape(devices, here, HEAD_DIM)
        acc[1] = value_sum.reshape(devices, here, HEAD_DIM)
        for d in range(chips):
            pair_out[h, d] = acc[:, 2 * d + 1 - lane].astype(BF16)
        go_pair(h).start()
        for d in range(chips):
            part[h, d] = acc[:, 2 * d + lane]

        @pl.when(h == me)
        def _():
            sink_in[me] = sink_part[h]

        @pl.when(h != me)
        def _():
            sink_send(h).start()

    def pair_sum(h):
        go_pair(h).wait_recv()
        for d in range(chips):
            part[h, d] = part[h, d] + pair_in[h, d].astype(F32)

    def pass_right(h):
        for d in range(last, 0, -1):

            @pl.when(d > chip)
            def _():
                @pl.when(chip == 0)
                def _():
                    right_out[h, d] = part[h, d].astype(BF16)

                @pl.when(chip > 0)
                def _():
                    sum_right(h, d).wait_recv()
                    right_out[h, d] = (part[h, d] + right_in[h, d].astype(F32)).astype(BF16)

                sum_right(h, d).start()

    def pass_left(h):
        for d in range(last):

            @pl.when(d < chip)
            def _():
                @pl.when(chip == last)
                def _():
                    left_out[h, d] = part[h, d].astype(BF16)

                @pl.when(chip < last)
                def _():
                    sum_left(h, d).wait_recv()
                    left_out[h, d] = (part[h, d] + left_in[h, d].astype(F32)).astype(BF16)

                sum_left(h, d).start()

    def finish(h):
        @pl.when(chip > 0)
        def _():
            sum_right(h, chip).wait_recv()
            part[h, chip] = part[h, chip] + right_in[h, chip].astype(F32)

        @pl.when(chip < last)
        def _():
            sum_left(h, chip).wait_recv()
            part[h, chip] = part[h, chip] + left_in[h, chip].astype(F32)

        cut = pl.ds(pl.multiple_of(h * HEAD_DIM, HEAD_DIM), HEAD_DIM)
        dk_ref[:, cut] = part[h, chip, 0].astype(BF16)
        dv_ref[:, cut] = part[h, chip, 1].astype(BF16)

    def sink_sum():
        for p in range(devices):

            @pl.when(p != me)
            def _():
                sink_recv(p).wait_recv()

        sink_dp[my_dp] = jnp.sum(sink_in[...], 0)
        for i in range(1, dps):
            across_dp(i, my_dp).start()

    def in_range(h):
        return (h >= 0) & (h < KV_HEADS)

    compute_at = chips
    pair_at = compute_at + 1
    finish_at = pair_at + last

    def tick(t, carry):
        def at(h, step, also=None):
            ready = in_range(h) if also is None else in_range(h) & also

            @pl.when(ready)
            def _():
                step(h)

        at(t + 2, send_own)
        for k in range(1, chips):
            at(t - k, lambda h: hand_on(h, k))
        at(t - pair_at, pair_sum)
        at(t - pair_at - chip, pass_right, chip < last)
        at(t - pair_at - (last - chip), pass_left, chip > 0)
        at(t - compute_at, compute)
        at(t - finish_at, finish)

        @pl.when(t == compute_at + KV_HEADS + 1)
        def _():
            sink_sum()

        return carry

    lax.fori_loop(0, finish_at + KV_HEADS, tick, 0)

    for i in range(1, dps):
        across_dp(i, lax.rem(my_dp - i + dps, dps)).wait_recv()
    total = sink_dp[0]
    for i in range(1, dps):
        total = total + sink_dp[i]
    ds_ref[...] = jnp.broadcast_to(jnp.sum(total, 1, keepdims=True), ds_ref.shape)

    def drain(h, carry):
        for k in range(last):

            @pl.when((chip >= k) & (chip < last))
            def _():
                go_right(h, k, chip - k).wait_send()

            @pl.when((chip + k <= last) & (chip > 0))
            def _():
                go_left(h, k, chip + k).wait_send()

        for z in range(chips):
            go_across(h, z, lane).wait_send()
        go_pair(h).wait_send()
        for d in range(chips):

            @pl.when(d > chip)
            def _():
                sum_right(h, d).wait_send()

            @pl.when(d < chip)
            def _():
                sum_left(h, d).wait_send()

        @pl.when(h != me)
        def _():
            sink_send(h).wait_send()

        return carry

    lax.fori_loop(0, KV_HEADS, drain, 0)
    for i in range(1, devices):
        logit(i, me).wait_send()
    for i in range(1, dps):
        across_dp(i, my_dp).wait_send()


def dense_shards(queries, key_states, value_states, sink_logit, out_grad, block_table):
    devices = lax.axis_size("seq")
    chips = devices // 2
    dps = lax.axis_size("dp")
    here = queries.shape[1]
    tile = (here, HEAD_DIM)
    sink_tile = jnp.pad(jnp.broadcast_to(sink_logit[:, None], (GROUP, HEAD_DIM)), ((0, 8 - GROUP), (0, 0)))
    dma = pltpu.SemaphoreType.DMA
    vmem = pl.BlockSpec(memory_space=pltpu.VMEM)
    flat = KV_HEADS * HEAD_DIM
    steps = [(KV_HEADS, chips - 1)] * 4 + [(KV_HEADS, chips)] * 2 + [(KV_HEADS,)] * 2
    steps += [(KV_HEADS, chips)] * 4 + [(devices,)] * 4 + [(dps,)] * 2
    per_head = pltpu.VMEM((KV_HEADS, chips, 2) + tile, BF16)
    query_grad, key_grad, value_grad, sink_sum = pl.pallas_call(
        dense_kernel,
        in_specs=[vmem] * 5,
        out_specs=[vmem] * 4,
        out_shape=[
            jax.ShapeDtypeStruct((here, HEADS * HEAD_DIM), BF16),
            jax.ShapeDtypeStruct((here, flat), BF16),
            jax.ShapeDtypeStruct((here, flat), BF16),
            jax.ShapeDtypeStruct((8, HEAD_DIM), F32),
        ],
        scratch_shapes=[
            pltpu.VMEM((2, KV_HEADS, devices) + tile, BF16),
            pltpu.VMEM((2, devices) + tile, F32),
            pltpu.VMEM((KV_HEADS, chips, 2) + tile, F32),
        ]
        + [per_head] * 6
        + [
            pltpu.VMEM((devices, 8, HEAD_DIM), F32),
            pltpu.VMEM((KV_HEADS, 8, HEAD_DIM), F32),
            pltpu.VMEM((devices, 8, HEAD_DIM), F32),
            pltpu.VMEM((dps, 8, HEAD_DIM), F32),
        ]
        + [dma(step) for step in steps],
        compiler_params=pltpu.CompilerParams(
            collective_id=0, has_side_effects=True, vmem_limit_bytes=52 * 2**20
        ),
    )(queries[0], out_grad[0], key_states[0], value_states[0], sink_tile)
    return query_grad[None], key_grad[None], value_grad[None], sink_sum[:GROUP, 0]


def shards(queries, key_states, value_states, sink_logit, out_grad, block_table):
    devices = lax.axis_size("seq")
    dense = queries.shape[1] == BLOCK and devices == KB and devices == KV_HEADS
    part = dense_shards if dense else sparse_shards
    return part(queries, key_states, value_states, sink_logit, out_grad, block_table)


def solution(mesh):
    in_specs = (
        P("dp", "seq", None),
        P("dp", "seq", None),
        P("dp", "seq", None),
        P("seq"),
        P("dp", "seq", None),
        P("seq", None, None),
    )
    out_specs = (P("dp", "seq", None), P("dp", "seq", None), P("dp", "seq", None), P("seq"))
    return jax.shard_map(shards, mesh=mesh, in_specs=in_specs, out_specs=out_specs, check_vma=False)
```

```python
import jax
import jax.numpy as jnp
from jax import lax
from jax.experimental import pallas as pl
from jax.experimental.pallas import tpu as pltpu
from jax.sharding import PartitionSpec as P

HEADS = 32
KV_HEADS = 8
HEAD_DIM = 128
BLOCK = 128
KB = 8


def sparse_shards(queries, key_states, value_states, sink_logit, out_grad, block_table):
    devices = lax.axis_size("seq")
    tokens_here = queries.shape[1]
    length = tokens_here * devices
    heads_here = HEADS // devices
    group = HEADS // KV_HEADS
    repeats = devices // KV_HEADS
    blocks = length // BLOCK
    scale = HEAD_DIM ** (-0.5)
    key_wide = jnp.repeat(key_states.reshape(1, tokens_here, KV_HEADS, 1, HEAD_DIM), group, axis=3)
    key_wide = key_wide.reshape(1, tokens_here, HEADS * HEAD_DIM)
    value_wide = jnp.repeat(
        value_states.reshape(1, tokens_here, KV_HEADS, 1, HEAD_DIM), group, axis=3
    )
    value_wide = value_wide.reshape(1, tokens_here, HEADS * HEAD_DIM)
    query_all, grad_all, key_all, value_all = (
        lax.all_to_all(queries, "seq", split_axis=2, concat_axis=1, tiled=True),
        lax.all_to_all(out_grad, "seq", split_axis=2, concat_axis=1, tiled=True),
        lax.all_to_all(key_wide, "seq", split_axis=2, concat_axis=1, tiled=True),
        lax.all_to_all(value_wide, "seq", split_axis=2, concat_axis=1, tiled=True),
    )
    key_rows = key_all[0, :, :HEAD_DIM]
    value_rows = value_all[0, :, :HEAD_DIM]
    group_blocks = max(4, blocks // 8)
    step_count = blocks // group_blocks
    query_steps = query_all.reshape(step_count, group_blocks, BLOCK, heads_here, HEAD_DIM)
    grad_steps = grad_all.reshape(step_count, group_blocks, BLOCK, heads_here, HEAD_DIM)
    table_steps = block_table.reshape(heads_here, step_count, group_blocks, KB).transpose(
        1, 0, 2, 3
    )
    key_table = key_rows.reshape(blocks, BLOCK, HEAD_DIM)
    value_table = value_rows.reshape(blocks, BLOCK, HEAD_DIM)
    sink_column = sink_logit[:, None, None]

    def advance(carry, items):
        key_acc, value_acc, sink_acc = carry
        query_group, grad_group, table_group = items
        key_pick = key_table[table_group].reshape(heads_here, group_blocks, KB * BLOCK, HEAD_DIM)
        value_pick = value_table[table_group].reshape(
            heads_here, group_blocks, KB * BLOCK, HEAD_DIM
        )
        scores = (
            jnp.einsum("gqhd,hgkd->hgqk", query_group, key_pick, preferred_element_type=jnp.float32)
            * scale
        )
        top = jnp.maximum(jnp.max(scores, -1), sink_column)
        weights = jnp.exp(scores - top[..., None])
        sink_weight = jnp.exp(sink_column - top)
        total = jnp.sum(weights, -1) + sink_weight
        probs = weights / total[..., None]
        sink_prob = sink_weight / total
        probs_low = probs.astype(jnp.bfloat16)
        attended = jnp.einsum(
            "hgqk,hgkd->gqhd", probs_low, value_pick, preferred_element_type=jnp.float32
        )
        delta_rows = jnp.sum(grad_group.astype(jnp.float32) * attended, -1)
        delta = jnp.transpose(delta_rows, (2, 0, 1))
        dprobs = jnp.einsum(
            "gqhd,hgkd->hgqk", grad_group, value_pick, preferred_element_type=jnp.float32
        )
        dscores = (probs * (dprobs - delta[..., None])).astype(jnp.bfloat16)
        query_part = (
            jnp.einsum("hgqk,hgkd->gqhd", dscores, key_pick, preferred_element_type=jnp.float32)
            * scale
        ).astype(jnp.bfloat16)
        key_terms = (
            jnp.einsum("hgqk,gqhd->hgkd", dscores, query_group, preferred_element_type=jnp.float32)
            * scale
        )
        value_terms = jnp.einsum(
            "hgqk,gqhd->hgkd", probs_low, grad_group, preferred_element_type=jnp.float32
        )
        flat_table = table_group.reshape(-1)
        key_acc = key_acc.at[flat_table].add(
            key_terms.reshape(heads_here * group_blocks * KB, BLOCK, HEAD_DIM)
        )
        value_acc = value_acc.at[flat_table].add(
            value_terms.reshape(heads_here * group_blocks * KB, BLOCK, HEAD_DIM)
        )
        sink_acc = sink_acc - jnp.sum(sink_prob * delta, axis=(1, 2))
        return ((key_acc, value_acc, sink_acc), query_part)

    start = (
        jnp.zeros((blocks, BLOCK, HEAD_DIM), jnp.float32),
        jnp.zeros((blocks, BLOCK, HEAD_DIM), jnp.float32),
        jnp.zeros((heads_here,), jnp.float32),
    )
    finished, query_parts = lax.scan(advance, start, (query_steps, grad_steps, table_steps))
    key_acc, value_acc, sink_acc = finished
    query_local = query_parts.reshape(1, length, heads_here * HEAD_DIM)
    query_grad = lax.all_to_all(query_local, "seq", split_axis=1, concat_axis=2, tiled=True)
    kv_terms = jnp.stack(
        [key_acc.reshape(length, HEAD_DIM), value_acc.reshape(length, HEAD_DIM)], 0
    )
    returned = lax.all_to_all(kv_terms, "seq", split_axis=1, concat_axis=2, tiled=True)
    kv_back = returned.reshape(2, tokens_here, KV_HEADS, repeats, HEAD_DIM).sum(3)
    kv_back = kv_back.reshape(2, tokens_here, KV_HEADS * HEAD_DIM)
    key_grad = kv_back[0:1].astype(jnp.bfloat16)
    value_grad = kv_back[1:2].astype(jnp.bfloat16)
    sink_grad = lax.psum(sink_acc, "dp")
    return (query_grad, key_grad, value_grad, sink_grad)


F32 = jnp.float32
BF16 = jnp.bfloat16
GROUP = HEADS // KV_HEADS
SCALE = HEAD_DIM ** (-0.5)


def group_terms(keys, values, queries, grads, sink_row):
    nt = (((1,), (1,)), ((), ()))
    tn = (((0,), (0,)), ((), ()))
    scores = lax.dot_general(keys, queries, nt, preferred_element_type=F32) * SCALE
    dprobs = lax.dot_general(values, grads, nt, preferred_element_type=F32)
    top = jnp.maximum(jnp.max(scores, 0, keepdims=True), sink_row)
    weights = jnp.exp(scores - top)
    sink_weight = jnp.exp(sink_row - top)
    inverse = 1.0 / (jnp.sum(weights, 0, keepdims=True) + sink_weight)
    probs = weights * inverse
    probs_low = probs.astype(BF16)
    delta = jnp.sum(probs_low.astype(F32) * dprobs, 0, keepdims=True)
    dscores = (probs * (dprobs - delta)).astype(BF16)
    value_terms = jnp.dot(probs_low, grads, preferred_element_type=F32)
    key_terms = jnp.dot(dscores, queries, preferred_element_type=F32)
    query_terms = lax.dot_general(keys, dscores, tn, preferred_element_type=F32)
    return key_terms, value_terms, query_terms.T * SCALE, -(sink_weight * inverse) * delta


def dense_kernel(
    q_ref, g_ref, k_ref, v_ref, sink_ref,
    dq_ref, dk_ref, dv_ref, ds_ref,
    kv_all, acc, part, pair_out, pair_in, right_out, right_in, left_out, left_in,
    sink_all, sink_part, sink_in, sink_dp, q_here, g_here,
    right_s, right_r, left_s, left_r, sib_s, sib_r, pair_s, pair_r,
    sumr_s, sumr_r, suml_s, suml_r, logit_s, logit_r, sg_s, sg_r, dp_s, dp_r, load_s, rows_s,
):
    devices = lax.axis_size("seq")
    chips = devices // 2
    last = chips - 1
    dps = lax.axis_size("dp")
    me = lax.axis_index("seq")
    my_dp = lax.axis_index("dp")
    chip = lax.div(me, 2)
    lane = lax.rem(me, 2)
    sibling = me + 1 - 2 * lane
    here = HEAD_DIM
    wide = GROUP * HEAD_DIM

    def remote(src, dst, send_sem, recv_sem, **target):
        return pltpu.make_async_remote_copy(
            src_ref=src, dst_ref=dst, send_sem=send_sem, recv_sem=recv_sem,
            device_id=target, device_id_type=pl.DeviceIdType.MESH,
        )

    def shard(h, z, which):
        return kv_all.at[:, h, 2 * z + which]

    def go_right(h, k, z):
        ref = shard(h, z, lane)
        return remote(ref, ref, right_s.at[h, k], right_r.at[h, k], seq=me + 2)

    def go_left(h, k, z):
        ref = shard(h, z, lane)
        return remote(ref, ref, left_s.at[h, k], left_r.at[h, k], seq=me - 2)

    def go_across(h, z, which):
        ref = shard(h, z, which)
        return remote(ref, ref, sib_s.at[h, z], sib_r.at[h, z], seq=sibling)

    def go_pair(h):
        return remote(pair_out.at[h], pair_in.at[h], pair_s.at[h], pair_r.at[h], seq=sibling)

    def sum_right(h, d):
        return remote(
            right_out.at[h, d], right_in.at[h, d], sumr_s.at[h, d], sumr_r.at[h, d], seq=me + 2
        )

    def sum_left(h, d):
        return remote(
            left_out.at[h, d], left_in.at[h, d], suml_s.at[h, d], suml_r.at[h, d], seq=me - 2
        )

    def logit(i, owner):
        ref = sink_all.at[owner]
        return remote(ref, ref, logit_s.at[i], logit_r.at[i], seq=lax.rem(me + i, devices))

    def sink_send(h):
        return remote(sink_part.at[h], sink_in.at[me], sg_s.at[h], sg_r.at[me], seq=h)

    def sink_recv(p):
        return remote(sink_part.at[p], sink_in.at[p], sg_s.at[p], sg_r.at[p], seq=p)

    def across_dp(i, owner):
        ref = sink_dp.at[owner]
        return remote(ref, ref, dp_s.at[i], dp_r.at[i], dp=lax.rem(my_dp + i, dps))

    barrier = pltpu.get_barrier_semaphore()
    for i in range(1, devices):
        pl.semaphore_signal(
            barrier, inc=1, device_id={"seq": lax.rem(me + i, devices)},
            device_id_type=pl.DeviceIdType.MESH,
        )
    for i in range(1, dps):
        pl.semaphore_signal(
            barrier, inc=1, device_id={"dp": lax.rem(my_dp + i, dps)},
            device_id_type=pl.DeviceIdType.MESH,
        )

    def load(which, h):
        ref = (k_ref, v_ref)[which]
        cut = pl.ds(pl.multiple_of(h * HEAD_DIM, HEAD_DIM), HEAD_DIM)
        return pltpu.make_async_copy(ref.at[:, cut], kv_all.at[which, h, me], load_s.at[which, h])

    rows = (
        pltpu.make_async_copy(q_ref, q_here, rows_s.at[0]),
        pltpu.make_async_copy(g_ref, g_here, rows_s.at[1]),
    )
    for h in range(KV_HEADS):
        for which in range(2):
            load(which, h).start()
    for copy in rows:
        copy.start()
    sink_all[me] = jnp.zeros_like(sink_all[me])
    for j in range(GROUP):
        sink_all[me, j : j + 1, :] = jnp.full((1, HEAD_DIM), sink_ref[j], F32)
    sink_part[...] = jnp.zeros_like(sink_part)
    pl.semaphore_wait(barrier, devices - 1 + dps - 1)

    def send_own(h):
        for which in range(2):
            load(which, h).wait()

        @pl.when(chip < last)
        def _():
            go_right(h, 0, chip).start()

        @pl.when(chip > 0)
        def _():
            go_left(h, 0, chip).start()

        go_across(h, chip, lane).start()

    send_own(0)
    for i in range(1, devices):
        logit(i, me).start()

    def ready_to_compute():
        for copy in rows:
            copy.wait()
        for i in range(1, devices):
            logit(i, lax.rem(me - i + devices, devices)).wait_recv()

    def hand_on(h, k):
        @pl.when(chip >= k)
        def _():
            go_right(h, k - 1, chip - k).wait_recv()
            if k < last:

                @pl.when(chip < last)
                def _():
                    go_right(h, k, chip - k).start()

            go_across(h, chip - k, lane).start()

        @pl.when(chip + k <= last)
        def _():
            go_left(h, k - 1, chip + k).wait_recv()
            if k < last:

                @pl.when(chip > 0)
                def _():
                    go_left(h, k, chip + k).start()

            go_across(h, chip + k, lane).start()

    def compute(h, half):
        if half == 0:
            for z in range(chips):
                go_across(h, z, 1 - lane).wait_recv()
        keys = kv_all[0, h].reshape(devices * here, HEAD_DIM)
        values = kv_all[1, h].reshape(devices * here, HEAD_DIM)
        heads = range(half * GROUP // 2, (half + 1) * GROUP // 2)
        cuts = [pl.ds(pl.multiple_of(h * wide + j * HEAD_DIM, HEAD_DIM), HEAD_DIM) for j in heads]
        queries = jnp.concatenate([q_here[:, cut] for cut in cuts], 0)
        grads = jnp.concatenate([g_here[:, cut] for cut in cuts], 0)
        sink_row = jnp.concatenate([sink_all[h, j : j + 1, :] for j in heads], 1)
        key_terms, value_terms, query_terms, sink_terms = group_terms(
            keys, values, queries, grads, sink_row
        )
        for i, j in enumerate(heads):
            span = slice(i * here, (i + 1) * here)
            dq_ref[:, cuts[i]] = query_terms[span].astype(BF16)
            sink_part[h, j : j + 1, :] = sink_terms[:, span]
        key_terms = (key_terms * SCALE).reshape(devices, here, HEAD_DIM)
        value_terms = value_terms.reshape(devices, here, HEAD_DIM)
        if half == 0:
            acc[0] = key_terms
            acc[1] = value_terms
            return
        acc[0] = acc[0] + key_terms
        acc[1] = acc[1] + value_terms
        for d in range(chips):
            pair_out[h, d] = acc[:, 2 * d + 1 - lane].astype(BF16)
        go_pair(h).start()
        for d in range(chips):
            part[h, d] = acc[:, 2 * d + lane]

        @pl.when(h == me)
        def _():
            sink_in[me] = sink_part[h]

        @pl.when(h != me)
        def _():
            sink_send(h).start()

    def pair_sum(h):
        go_pair(h).wait_recv()
        for d in range(chips):
            part[h, d] = part[h, d] + pair_in[h, d].astype(F32)

    def pass_right(h):
        for d in range(last, 0, -1):

            @pl.when(d > chip)
            def _():
                @pl.when(chip == 0)
                def _():
                    right_out[h, d] = part[h, d].astype(BF16)

                @pl.when(chip > 0)
                def _():
                    sum_right(h, d).wait_recv()
                    right_out[h, d] = (part[h, d] + right_in[h, d].astype(F32)).astype(BF16)

                sum_right(h, d).start()

    def pass_left(h):
        for d in range(last):

            @pl.when(d < chip)
            def _():
                @pl.when(chip == last)
                def _():
                    left_out[h, d] = part[h, d].astype(BF16)

                @pl.when(chip < last)
                def _():
                    sum_left(h, d).wait_recv()
                    left_out[h, d] = (part[h, d] + left_in[h, d].astype(F32)).astype(BF16)

                sum_left(h, d).start()

    def finish(h):
        @pl.when(chip > 0)
        def _():
            sum_right(h, chip).wait_recv()
            part[h, chip] = part[h, chip] + right_in[h, chip].astype(F32)

        @pl.when(chip < last)
        def _():
            sum_left(h, chip).wait_recv()
            part[h, chip] = part[h, chip] + left_in[h, chip].astype(F32)

        cut = pl.ds(pl.multiple_of(h * HEAD_DIM, HEAD_DIM), HEAD_DIM)
        dk_ref[:, cut] = part[h, chip, 0].astype(BF16)
        dv_ref[:, cut] = part[h, chip, 1].astype(BF16)

    def sink_sum():
        for p in range(devices):

            @pl.when(p != me)
            def _():
                sink_recv(p).wait_recv()

        sink_dp[my_dp] = jnp.sum(sink_in[...], 0)
        for i in range(1, dps):
            across_dp(i, my_dp).start()

    def in_range(h):
        return (h >= 0) & (h < KV_HEADS)

    compute_at = chips
    pair_at = compute_at + 1
    finish_at = pair_at + 2 * last

    def tick(t, carry):
        def at(h, step, also=None):
            ready = in_range(h) if also is None else in_range(h) & also

            @pl.when(ready)
            def _():
                step(h)

        pl.when(t == compute_at)(ready_to_compute)
        at(t - compute_at, lambda h: compute(h, 0))
        at(t - pair_at, pair_sum)
        at(t - pair_at - chip, pass_right, chip < last)
        at(t - 3, lambda h: hand_on(h, 3))
        at(t - compute_at, lambda h: compute(h, 1))
        at(t - 2, lambda h: hand_on(h, 2))
        at(t - pair_at - (last - chip), pass_left, chip > 0)
        at(t - 1, lambda h: hand_on(h, 1))
        at(t + 1, send_own)
        at(t - finish_at, finish)
        pl.when(t == compute_at + KV_HEADS + 1)(sink_sum)
        return carry

    lax.fori_loop(0, finish_at + KV_HEADS, tick, 0)

    for i in range(1, dps):
        across_dp(i, lax.rem(my_dp - i + dps, dps)).wait_recv()
    total = sink_dp[0]
    for i in range(1, dps):
        total = total + sink_dp[i]
    ds_ref[...] = jnp.broadcast_to(jnp.sum(total, 1, keepdims=True), ds_ref.shape)

    def drain(h, carry):
        for k in range(last):

            @pl.when((chip >= k) & (chip < last))
            def _():
                go_right(h, k, chip - k).wait_send()

            @pl.when((chip + k <= last) & (chip > 0))
            def _():
                go_left(h, k, chip + k).wait_send()

        for z in range(chips):
            go_across(h, z, lane).wait_send()
        go_pair(h).wait_send()
        for d in range(chips):

            @pl.when(d > chip)
            def _():
                sum_right(h, d).wait_send()

            @pl.when(d < chip)
            def _():
                sum_left(h, d).wait_send()

        @pl.when(h != me)
        def _():
            sink_send(h).wait_send()

        return carry

    lax.fori_loop(0, KV_HEADS, drain, 0)
    for i in range(1, devices):
        logit(i, me).wait_send()
    for i in range(1, dps):
        across_dp(i, my_dp).wait_send()


def dense_shards(queries, key_states, value_states, sink_logit, out_grad, block_table):
    devices = lax.axis_size("seq")
    chips = devices // 2
    dps = lax.axis_size("dp")
    here = queries.shape[1]
    tile = (here, HEAD_DIM)
    dma = pltpu.SemaphoreType.DMA
    vmem = pl.BlockSpec(memory_space=pltpu.VMEM)
    flat = KV_HEADS * HEAD_DIM
    steps = [(KV_HEADS, chips - 1)] * 4 + [(KV_HEADS, chips)] * 2 + [(KV_HEADS,)] * 2
    steps += [(KV_HEADS, chips)] * 4 + [(devices,)] * 4 + [(dps,)] * 2 + [(2, KV_HEADS), (2,)]
    per_head = pltpu.VMEM((KV_HEADS, chips, 2) + tile, BF16)
    query_grad, key_grad, value_grad, sink_sum = pl.pallas_call(
        dense_kernel,
        in_specs=[pl.BlockSpec(memory_space=pltpu.HBM)] * 4
        + [pl.BlockSpec(memory_space=pltpu.SMEM)],
        out_specs=[vmem] * 4,
        out_shape=[
            jax.ShapeDtypeStruct((here, HEADS * HEAD_DIM), BF16),
            jax.ShapeDtypeStruct((here, flat), BF16),
            jax.ShapeDtypeStruct((here, flat), BF16),
            jax.ShapeDtypeStruct((8, HEAD_DIM), F32),
        ],
        scratch_shapes=[
            pltpu.VMEM((2, KV_HEADS, devices) + tile, BF16),
            pltpu.VMEM((2, devices) + tile, F32),
            pltpu.VMEM((KV_HEADS, chips, 2) + tile, F32),
        ]
        + [per_head] * 6
        + [
            pltpu.VMEM((devices, 8, HEAD_DIM), F32),
            pltpu.VMEM((KV_HEADS, 8, HEAD_DIM), F32),
            pltpu.VMEM((devices, 8, HEAD_DIM), F32),
            pltpu.VMEM((dps, 8, HEAD_DIM), F32),
            pltpu.VMEM((here, HEADS * HEAD_DIM), BF16),
            pltpu.VMEM((here, HEADS * HEAD_DIM), BF16),
        ]
        + [dma(step) for step in steps],
        compiler_params=pltpu.CompilerParams(
            collective_id=0, has_side_effects=True, vmem_limit_bytes=62 * 2**20
        ),
    )(queries[0], out_grad[0], key_states[0], value_states[0], sink_logit)
    return query_grad[None], key_grad[None], value_grad[None], sink_sum[:GROUP, 0]


def shards(queries, key_states, value_states, sink_logit, out_grad, block_table):
    devices = lax.axis_size("seq")
    dense = queries.shape[1] == BLOCK and devices == KB and devices == KV_HEADS
    part = dense_shards if dense else sparse_shards
    return part(queries, key_states, value_states, sink_logit, out_grad, block_table)


def solution(mesh):
    in_specs = (
        P("dp", "seq", None),
        P("dp", "seq", None),
        P("dp", "seq", None),
        P("seq"),
        P("dp", "seq", None),
        P("seq", None, None),
    )
    out_specs = (P("dp", "seq", None), P("dp", "seq", None), P("dp", "seq", None), P("seq"))
    return jax.shard_map(shards, mesh=mesh, in_specs=in_specs, out_specs=out_specs, check_vma=False)
```

```python
import jax
import jax.numpy as jnp
from jax import lax
from jax.experimental import pallas as pl
from jax.experimental.pallas import tpu as pltpu
from jax.sharding import PartitionSpec as P

HEADS = 32
KV_HEADS = 8
HEAD_DIM = 128
BLOCK = 128
KB = 8


def sparse_shards(queries, key_states, value_states, sink_logit, out_grad, block_table):
    devices = lax.axis_size("seq")
    tokens_here = queries.shape[1]
    length = tokens_here * devices
    heads_here = HEADS // devices
    group = HEADS // KV_HEADS
    repeats = devices // KV_HEADS
    blocks = length // BLOCK
    scale = HEAD_DIM ** (-0.5)
    key_wide = jnp.repeat(key_states.reshape(1, tokens_here, KV_HEADS, 1, HEAD_DIM), group, axis=3)
    key_wide = key_wide.reshape(1, tokens_here, HEADS * HEAD_DIM)
    value_wide = jnp.repeat(
        value_states.reshape(1, tokens_here, KV_HEADS, 1, HEAD_DIM), group, axis=3
    )
    value_wide = value_wide.reshape(1, tokens_here, HEADS * HEAD_DIM)
    query_all, grad_all, key_all, value_all = (
        lax.all_to_all(queries, "seq", split_axis=2, concat_axis=1, tiled=True),
        lax.all_to_all(out_grad, "seq", split_axis=2, concat_axis=1, tiled=True),
        lax.all_to_all(key_wide, "seq", split_axis=2, concat_axis=1, tiled=True),
        lax.all_to_all(value_wide, "seq", split_axis=2, concat_axis=1, tiled=True),
    )
    key_rows = key_all[0, :, :HEAD_DIM]
    value_rows = value_all[0, :, :HEAD_DIM]
    group_blocks = max(4, blocks // 8)
    step_count = blocks // group_blocks
    query_steps = query_all.reshape(step_count, group_blocks, BLOCK, heads_here, HEAD_DIM)
    grad_steps = grad_all.reshape(step_count, group_blocks, BLOCK, heads_here, HEAD_DIM)
    table_steps = block_table.reshape(heads_here, step_count, group_blocks, KB).transpose(
        1, 0, 2, 3
    )
    key_table = key_rows.reshape(blocks, BLOCK, HEAD_DIM)
    value_table = value_rows.reshape(blocks, BLOCK, HEAD_DIM)
    sink_column = sink_logit[:, None, None]

    def advance(carry, items):
        key_acc, value_acc, sink_acc = carry
        query_group, grad_group, table_group = items
        key_pick = key_table[table_group].reshape(heads_here, group_blocks, KB * BLOCK, HEAD_DIM)
        value_pick = value_table[table_group].reshape(
            heads_here, group_blocks, KB * BLOCK, HEAD_DIM
        )
        scores = (
            jnp.einsum("gqhd,hgkd->hgqk", query_group, key_pick, preferred_element_type=jnp.float32)
            * scale
        )
        top = jnp.maximum(jnp.max(scores, -1), sink_column)
        weights = jnp.exp(scores - top[..., None])
        sink_weight = jnp.exp(sink_column - top)
        total = jnp.sum(weights, -1) + sink_weight
        probs = weights / total[..., None]
        sink_prob = sink_weight / total
        probs_low = probs.astype(jnp.bfloat16)
        attended = jnp.einsum(
            "hgqk,hgkd->gqhd", probs_low, value_pick, preferred_element_type=jnp.float32
        )
        delta_rows = jnp.sum(grad_group.astype(jnp.float32) * attended, -1)
        delta = jnp.transpose(delta_rows, (2, 0, 1))
        dprobs = jnp.einsum(
            "gqhd,hgkd->hgqk", grad_group, value_pick, preferred_element_type=jnp.float32
        )
        dscores = (probs * (dprobs - delta[..., None])).astype(jnp.bfloat16)
        query_part = (
            jnp.einsum("hgqk,hgkd->gqhd", dscores, key_pick, preferred_element_type=jnp.float32)
            * scale
        ).astype(jnp.bfloat16)
        key_terms = (
            jnp.einsum("hgqk,gqhd->hgkd", dscores, query_group, preferred_element_type=jnp.float32)
            * scale
        )
        value_terms = jnp.einsum(
            "hgqk,gqhd->hgkd", probs_low, grad_group, preferred_element_type=jnp.float32
        )
        flat_table = table_group.reshape(-1)
        key_acc = key_acc.at[flat_table].add(
            key_terms.reshape(heads_here * group_blocks * KB, BLOCK, HEAD_DIM)
        )
        value_acc = value_acc.at[flat_table].add(
            value_terms.reshape(heads_here * group_blocks * KB, BLOCK, HEAD_DIM)
        )
        sink_acc = sink_acc - jnp.sum(sink_prob * delta, axis=(1, 2))
        return ((key_acc, value_acc, sink_acc), query_part)

    start = (
        jnp.zeros((blocks, BLOCK, HEAD_DIM), jnp.float32),
        jnp.zeros((blocks, BLOCK, HEAD_DIM), jnp.float32),
        jnp.zeros((heads_here,), jnp.float32),
    )
    finished, query_parts = lax.scan(advance, start, (query_steps, grad_steps, table_steps))
    key_acc, value_acc, sink_acc = finished
    query_local = query_parts.reshape(1, length, heads_here * HEAD_DIM)
    query_grad = lax.all_to_all(query_local, "seq", split_axis=1, concat_axis=2, tiled=True)
    kv_terms = jnp.stack(
        [key_acc.reshape(length, HEAD_DIM), value_acc.reshape(length, HEAD_DIM)], 0
    )
    returned = lax.all_to_all(kv_terms, "seq", split_axis=1, concat_axis=2, tiled=True)
    kv_back = returned.reshape(2, tokens_here, KV_HEADS, repeats, HEAD_DIM).sum(3)
    kv_back = kv_back.reshape(2, tokens_here, KV_HEADS * HEAD_DIM)
    key_grad = kv_back[0:1].astype(jnp.bfloat16)
    value_grad = kv_back[1:2].astype(jnp.bfloat16)
    sink_grad = lax.psum(sink_acc, "dp")
    return (query_grad, key_grad, value_grad, sink_grad)


F32 = jnp.float32
BF16 = jnp.bfloat16
GROUP = HEADS // KV_HEADS
SCALE = HEAD_DIM ** (-0.5)
LOG2E = 1.4426950408889634


def group_terms(keys, values, queries, grads, sink_row):
    nt = (((1,), (1,)), ((), ()))
    tn = (((0,), (0,)), ((), ()))
    scores = lax.dot_general(keys, queries, nt, preferred_element_type=F32)
    dprobs = lax.dot_general(values, grads, nt, preferred_element_type=F32)
    top = jnp.maximum(jnp.max(scores, 0, keepdims=True) * SCALE, sink_row)
    weights = jnp.exp2(scores * (SCALE * LOG2E) - top * LOG2E)
    sink_weight = jnp.exp(sink_row - top)
    inverse = 1.0 / (jnp.sum(weights, 0, keepdims=True) + sink_weight)
    probs = weights * inverse
    probs_low = probs.astype(BF16)
    delta = jnp.sum(probs_low.astype(F32) * dprobs, 0, keepdims=True)
    dscores = (probs * (dprobs - delta)).astype(BF16)
    value_terms = jnp.dot(probs_low, grads, preferred_element_type=F32)
    key_terms = jnp.dot(dscores, queries, preferred_element_type=F32)
    query_terms = lax.dot_general(keys, dscores, tn, preferred_element_type=F32)
    return key_terms, value_terms, query_terms.T * SCALE, -(sink_weight * inverse) * delta


def dense_kernel(
    q_ref, g_ref, k_ref, v_ref, sink_ref,
    dq_ref, dk_ref, dv_ref, ds_ref,
    kv_all, acc, part, pair_out, pair_in, right_out, right_in, left_out, left_in,
    sink_all, sink_part, sink_in, sink_dp, q_here, g_here, dq_here, dk_here, dv_here,
    right_s, right_r, left_s, left_r, sib_s, sib_r, pair_s, pair_r,
    sumr_s, sumr_r, suml_s, suml_r, logit_s, logit_r, sg_s, sg_r, dp_s, dp_r, load_s, rows_s, leave_s,
):
    devices = lax.axis_size("seq")
    chips = devices // 2
    last = chips - 1
    dps = lax.axis_size("dp")
    me = lax.axis_index("seq")
    my_dp = lax.axis_index("dp")
    chip = lax.div(me, 2)
    lane = lax.rem(me, 2)
    sibling = me + 1 - 2 * lane
    here = HEAD_DIM
    wide = GROUP * HEAD_DIM

    def remote(src, dst, send_sem, recv_sem, **target):
        return pltpu.make_async_remote_copy(
            src_ref=src, dst_ref=dst, send_sem=send_sem, recv_sem=recv_sem,
            device_id=target, device_id_type=pl.DeviceIdType.MESH,
        )

    def shard(h, z, which):
        return kv_all.at[:, h, 2 * z + which]

    def go_right(h, k, z):
        ref = shard(h, z, lane)
        return remote(ref, ref, right_s.at[h, k], right_r.at[h, k], seq=me + 2)

    def go_left(h, k, z):
        ref = shard(h, z, lane)
        return remote(ref, ref, left_s.at[h, k], left_r.at[h, k], seq=me - 2)

    def go_across(h, z, which):
        ref = shard(h, z, which)
        return remote(ref, ref, sib_s.at[h, z], sib_r.at[h, z], seq=sibling)

    def go_pair(h):
        return remote(pair_out.at[h], pair_in.at[h], pair_s.at[h], pair_r.at[h], seq=sibling)

    def sum_right(h, d):
        return remote(
            right_out.at[h, d], right_in.at[h, d], sumr_s.at[h, d], sumr_r.at[h, d], seq=me + 2
        )

    def sum_left(h, d):
        return remote(
            left_out.at[h, d], left_in.at[h, d], suml_s.at[h, d], suml_r.at[h, d], seq=me - 2
        )

    def logit(i, owner):
        ref = sink_all.at[owner]
        return remote(ref, ref, logit_s.at[i], logit_r.at[i], seq=lax.rem(me + i, devices))

    def sink_send(h):
        return remote(sink_part.at[h], sink_in.at[me], sg_s.at[h], sg_r.at[me], seq=h)

    def sink_recv(p):
        return remote(sink_part.at[p], sink_in.at[p], sg_s.at[p], sg_r.at[p], seq=p)

    def across_dp(i, owner):
        ref = sink_dp.at[owner]
        return remote(ref, ref, dp_s.at[i], dp_r.at[i], dp=lax.rem(my_dp + i, dps))

    barrier = pltpu.get_barrier_semaphore()
    for i in range(1, devices):
        pl.semaphore_signal(
            barrier, inc=1, device_id={"seq": lax.rem(me + i, devices)},
            device_id_type=pl.DeviceIdType.MESH,
        )
    for i in range(1, dps):
        pl.semaphore_signal(
            barrier, inc=1, device_id={"dp": lax.rem(my_dp + i, dps)},
            device_id_type=pl.DeviceIdType.MESH,
        )

    def load(which, h):
        ref = (k_ref, v_ref)[which]
        cut = pl.ds(pl.multiple_of(h * HEAD_DIM, HEAD_DIM), HEAD_DIM)
        return pltpu.make_async_copy(ref.at[:, cut], kv_all.at[which, h, me], load_s.at[which, h])

    rows = (
        pltpu.make_async_copy(q_ref, q_here, rows_s.at[0]),
        pltpu.make_async_copy(g_ref, g_here, rows_s.at[1]),
    )
    for h in range(KV_HEADS):
        for which in range(2):
            load(which, h).start()
    for copy in rows:
        copy.start()
    sink_all[me] = jnp.zeros_like(sink_all[me])
    for j in range(GROUP):
        sink_all[me, j : j + 1, :] = jnp.full((1, HEAD_DIM), sink_ref[j], F32)
    sink_part[...] = jnp.zeros_like(sink_part)
    pl.semaphore_wait(barrier, devices - 1 + dps - 1)

    def leave(which, h):
        held, out = ((dq_here, dq_ref), (dk_here, dk_ref), (dv_here, dv_ref))[which]
        size = wide if which == 0 else HEAD_DIM
        cut = pl.ds(pl.multiple_of(h * size, size), size)
        return pltpu.make_async_copy(held.at[:, cut], out.at[:, cut], leave_s.at[which, h])

    def send_own(h):
        for which in range(2):
            load(which, h).wait()

        @pl.when(chip < last)
        def _():
            go_right(h, 0, chip).start()

        @pl.when(chip > 0)
        def _():
            go_left(h, 0, chip).start()

        go_across(h, chip, lane).start()

    send_own(0)
    for i in range(1, devices):
        logit(i, me).start()

    def ready_to_compute():
        for copy in rows:
            copy.wait()
        for i in range(1, devices):
            logit(i, lax.rem(me - i + devices, devices)).wait_recv()

    def hand_on(h, k):
        @pl.when(chip >= k)
        def _():
            go_right(h, k - 1, chip - k).wait_recv()
            if k < last:

                @pl.when(chip < last)
                def _():
                    go_right(h, k, chip - k).start()

            go_across(h, chip - k, lane).start()

        @pl.when(chip + k <= last)
        def _():
            go_left(h, k - 1, chip + k).wait_recv()
            if k < last:

                @pl.when(chip > 0)
                def _():
                    go_left(h, k, chip + k).start()

            go_across(h, chip + k, lane).start()

    def compute(h):
        for z in range(chips):
            go_across(h, z, 1 - lane).wait_recv()
        keys = kv_all[0, h].reshape(devices * here, HEAD_DIM)
        values = kv_all[1, h].reshape(devices * here, HEAD_DIM)
        key_sum = value_sum = None
        for half in range(2):
            heads = range(half * GROUP // 2, (half + 1) * GROUP // 2)
            cuts = [pl.ds(pl.multiple_of(h * wide + j * HEAD_DIM, HEAD_DIM), HEAD_DIM) for j in heads]
            queries = jnp.concatenate([q_here[:, cut] for cut in cuts], 0)
            grads = jnp.concatenate([g_here[:, cut] for cut in cuts], 0)
            sink_row = jnp.concatenate([sink_all[h, j : j + 1, :] for j in heads], 1)
            key_terms, value_terms, query_terms, sink_terms = group_terms(
                keys, values, queries, grads, sink_row
            )
            for i, j in enumerate(heads):
                span = slice(i * here, (i + 1) * here)
                dq_here[:, cuts[i]] = query_terms[span].astype(BF16)
                sink_part[h, j : j + 1, :] = sink_terms[:, span]
            key_sum = key_terms if half == 0 else key_sum + key_terms
            value_sum = value_terms if half == 0 else value_sum + value_terms
        acc[0] = (key_sum * SCALE).reshape(devices, here, HEAD_DIM)
        acc[1] = value_sum.reshape(devices, here, HEAD_DIM)
        for d in range(chips):
            pair_out[h, d] = acc[:, 2 * d + 1 - lane].astype(BF16)
        go_pair(h).start()
        leave(0, h).start()
        for d in range(chips):
            part[h, d] = acc[:, 2 * d + lane]

        @pl.when(h == me)
        def _():
            sink_in[me] = sink_part[h]

        @pl.when(h != me)
        def _():
            sink_send(h).start()

    def pair_sum(h):
        go_pair(h).wait_recv()
        for d in range(chips):
            part[h, d] = part[h, d] + pair_in[h, d].astype(F32)

    def pass_right(h):
        for d in range(last, 0, -1):

            @pl.when(d > chip)
            def _():
                @pl.when(chip == 0)
                def _():
                    right_out[h, d] = part[h, d].astype(BF16)

                @pl.when(chip > 0)
                def _():
                    sum_right(h, d).wait_recv()
                    right_out[h, d] = (part[h, d] + right_in[h, d].astype(F32)).astype(BF16)

                sum_right(h, d).start()

    def pass_left(h):
        for d in range(last):

            @pl.when(d < chip)
            def _():
                @pl.when(chip == last)
                def _():
                    left_out[h, d] = part[h, d].astype(BF16)

                @pl.when(chip < last)
                def _():
                    sum_left(h, d).wait_recv()
                    left_out[h, d] = (part[h, d] + left_in[h, d].astype(F32)).astype(BF16)

                sum_left(h, d).start()

    def finish(h):
        @pl.when(chip > 0)
        def _():
            sum_right(h, chip).wait_recv()
            part[h, chip] = part[h, chip] + right_in[h, chip].astype(F32)

        @pl.when(chip < last)
        def _():
            sum_left(h, chip).wait_recv()
            part[h, chip] = part[h, chip] + left_in[h, chip].astype(F32)

        cut = pl.ds(pl.multiple_of(h * HEAD_DIM, HEAD_DIM), HEAD_DIM)
        dk_here[:, cut] = part[h, chip, 0].astype(BF16)
        dv_here[:, cut] = part[h, chip, 1].astype(BF16)
        leave(1, h).start()
        leave(2, h).start()

    def sink_sum():
        for p in range(devices):

            @pl.when(p != me)
            def _():
                sink_recv(p).wait_recv()

        sink_dp[my_dp] = jnp.sum(sink_in[...], 0)
        for i in range(1, dps):
            across_dp(i, my_dp).start()

    def in_range(h):
        return (h >= 0) & (h < KV_HEADS)

    compute_at = chips
    pair_at = compute_at + 1
    finish_at = pair_at + 2 * last - 1

    def tick(t, carry):
        def at(h, step, also=None):
            ready = in_range(h) if also is None else in_range(h) & also

            @pl.when(ready)
            def _():
                step(h)

        pl.when(t == compute_at)(ready_to_compute)
        at(t - compute_at, compute)
        at(t - pair_at, pair_sum)
        at(t - 3, lambda h: hand_on(h, 3))
        at(t - pair_at - chip, pass_right, chip < last)
        at(t - pair_at - (last - chip), pass_left, chip > 0)
        at(t - 2, lambda h: hand_on(h, 2))
        at(t - 1, lambda h: hand_on(h, 1))
        at(t + 1, send_own)
        at(t - finish_at, finish)
        pl.when(t == compute_at + KV_HEADS + 1)(sink_sum)
        return carry

    lax.fori_loop(0, finish_at + KV_HEADS, tick, 0)

    for i in range(1, dps):
        across_dp(i, lax.rem(my_dp - i + dps, dps)).wait_recv()
    total = sink_dp[0]
    for i in range(1, dps):
        total = total + sink_dp[i]
    for j in range(GROUP):
        ds_ref[j] = jnp.sum(total[j : j + 1])

    def drain(h, carry):
        for k in range(last):

            @pl.when((chip >= k) & (chip < last))
            def _():
                go_right(h, k, chip - k).wait_send()

            @pl.when((chip + k <= last) & (chip > 0))
            def _():
                go_left(h, k, chip + k).wait_send()

        for z in range(chips):
            go_across(h, z, lane).wait_send()
        go_pair(h).wait_send()
        for which in range(3):
            leave(which, h).wait()
        for d in range(chips):

            @pl.when(d > chip)
            def _():
                sum_right(h, d).wait_send()

            @pl.when(d < chip)
            def _():
                sum_left(h, d).wait_send()

        @pl.when(h != me)
        def _():
            sink_send(h).wait_send()

        return carry

    lax.fori_loop(0, KV_HEADS, drain, 0)
    for i in range(1, devices):
        logit(i, me).wait_send()
    for i in range(1, dps):
        across_dp(i, my_dp).wait_send()


def place_kernel(*refs):
    held, out, sems = refs[:4], refs[4:8], refs[8]
    rows = held[0].shape[0] // 4
    pairs = [(held[0].at[pl.ds(i * rows, rows)], out[0].at[pl.ds(i * rows, rows)]) for i in range(4)]
    pairs += [(held[1], out[1]), (held[2], out[2])]
    copies = [pltpu.make_async_copy(*pair, sems.at[i]) for i, pair in enumerate(pairs)]
    for copy in copies:
        copy.start()
    for j in range(GROUP):
        out[3][j] = held[3][j]
    for copy in copies:
        copy.wait()


def dense_shards(queries, key_states, value_states, sink_logit, out_grad, block_table):
    devices = lax.axis_size("seq")
    chips = devices // 2
    dps = lax.axis_size("dp")
    here = queries.shape[1]
    tile = (here, HEAD_DIM)
    dma = pltpu.SemaphoreType.DMA
    hbm = pl.BlockSpec(memory_space=pltpu.HBM)
    smem = pl.BlockSpec(memory_space=pltpu.SMEM)
    flat = KV_HEADS * HEAD_DIM
    steps = [(KV_HEADS, chips - 1)] * 4 + [(KV_HEADS, chips)] * 2 + [(KV_HEADS,)] * 2
    steps += [(KV_HEADS, chips)] * 4 + [(devices,)] * 4 + [(dps,)] * 2 + [(2, KV_HEADS), (2,), (3, KV_HEADS)]
    per_head = pltpu.VMEM((KV_HEADS, chips, 2) + tile, BF16)
    results = [
        jax.ShapeDtypeStruct((here, HEADS * HEAD_DIM), BF16),
        jax.ShapeDtypeStruct((here, flat), BF16),
        jax.ShapeDtypeStruct((here, flat), BF16),
        jax.ShapeDtypeStruct((GROUP,), F32),
    ]
    held = pl.pallas_call(
        dense_kernel,
        in_specs=[hbm] * 4 + [smem],
        out_specs=[hbm] * 3 + [smem],
        out_shape=results,
        scratch_shapes=[
            pltpu.VMEM((2, KV_HEADS, devices) + tile, BF16),
            pltpu.VMEM((2, devices) + tile, F32),
            pltpu.VMEM((KV_HEADS, chips, 2) + tile, F32),
        ]
        + [per_head] * 6
        + [
            pltpu.VMEM((devices, 8, HEAD_DIM), F32),
            pltpu.VMEM((KV_HEADS, 8, HEAD_DIM), F32),
            pltpu.VMEM((devices, 8, HEAD_DIM), F32),
            pltpu.VMEM((dps, 8, HEAD_DIM), F32),
        ]
        + [pltpu.VMEM((here, HEADS * HEAD_DIM), BF16)] * 3
        + [pltpu.VMEM((here, flat), BF16)] * 2
        + [dma(step) for step in steps],
        compiler_params=pltpu.CompilerParams(
            collective_id=0, has_side_effects=True, vmem_limit_bytes=62 * 2**20
        ),
    )(queries[0], out_grad[0], key_states[0], value_states[0], sink_logit)
    query_grad, key_grad, value_grad, sink_grad = pl.pallas_call(
        place_kernel,
        in_specs=[hbm] * 3 + [smem],
        out_specs=[hbm] * 3 + [smem],
        out_shape=results,
        scratch_shapes=[dma((6,))],
        compiler_params=pltpu.CompilerParams(vmem_limit_bytes=62 * 2**20),
    )(*held)
    return query_grad[None], key_grad[None], value_grad[None], sink_grad


def shards(queries, key_states, value_states, sink_logit, out_grad, block_table):
    devices = lax.axis_size("seq")
    dense = queries.shape[1] == BLOCK and devices == KB and devices == KV_HEADS
    part = dense_shards if dense else sparse_shards
    return part(queries, key_states, value_states, sink_logit, out_grad, block_table)


def solution(mesh):
    in_specs = (
        P("dp", "seq", None),
        P("dp", "seq", None),
        P("dp", "seq", None),
        P("seq"),
        P("dp", "seq", None),
        P("seq", None, None),
    )
    out_specs = (P("dp", "seq", None), P("dp", "seq", None), P("dp", "seq", None), P("seq"))
    return jax.shard_map(shards, mesh=mesh, in_specs=in_specs, out_specs=out_specs, check_vma=False)
```

```python
import jax
import jax.numpy as jnp
from jax import lax
from jax.experimental import pallas as pl
from jax.experimental.pallas import tpu as pltpu
from jax.sharding import PartitionSpec as P

HEADS = 32
KV_HEADS = 8
HEAD_DIM = 128
BLOCK = 128
KB = 8


def sparse_shards(queries, key_states, value_states, sink_logit, out_grad, block_table):
    devices = lax.axis_size("seq")
    tokens_here = queries.shape[1]
    length = tokens_here * devices
    heads_here = HEADS // devices
    group = HEADS // KV_HEADS
    repeats = devices // KV_HEADS
    blocks = length // BLOCK
    scale = HEAD_DIM ** (-0.5)
    key_wide = jnp.repeat(key_states.reshape(1, tokens_here, KV_HEADS, 1, HEAD_DIM), group, axis=3)
    key_wide = key_wide.reshape(1, tokens_here, HEADS * HEAD_DIM)
    value_wide = jnp.repeat(
        value_states.reshape(1, tokens_here, KV_HEADS, 1, HEAD_DIM), group, axis=3
    )
    value_wide = value_wide.reshape(1, tokens_here, HEADS * HEAD_DIM)
    query_all, grad_all, key_all, value_all = (
        lax.all_to_all(queries, "seq", split_axis=2, concat_axis=1, tiled=True),
        lax.all_to_all(out_grad, "seq", split_axis=2, concat_axis=1, tiled=True),
        lax.all_to_all(key_wide, "seq", split_axis=2, concat_axis=1, tiled=True),
        lax.all_to_all(value_wide, "seq", split_axis=2, concat_axis=1, tiled=True),
    )
    key_rows = key_all[0, :, :HEAD_DIM]
    value_rows = value_all[0, :, :HEAD_DIM]
    group_blocks = max(4, blocks // 8)
    step_count = blocks // group_blocks
    query_steps = query_all.reshape(step_count, group_blocks, BLOCK, heads_here, HEAD_DIM)
    grad_steps = grad_all.reshape(step_count, group_blocks, BLOCK, heads_here, HEAD_DIM)
    table_steps = block_table.reshape(heads_here, step_count, group_blocks, KB).transpose(
        1, 0, 2, 3
    )
    key_table = key_rows.reshape(blocks, BLOCK, HEAD_DIM)
    value_table = value_rows.reshape(blocks, BLOCK, HEAD_DIM)
    sink_column = sink_logit[:, None, None]

    def advance(carry, items):
        key_acc, value_acc, sink_acc = carry
        query_group, grad_group, table_group = items
        key_pick = key_table[table_group].reshape(heads_here, group_blocks, KB * BLOCK, HEAD_DIM)
        value_pick = value_table[table_group].reshape(
            heads_here, group_blocks, KB * BLOCK, HEAD_DIM
        )
        scores = (
            jnp.einsum("gqhd,hgkd->hgqk", query_group, key_pick, preferred_element_type=jnp.float32)
            * scale
        )
        top = jnp.maximum(jnp.max(scores, -1), sink_column)
        weights = jnp.exp(scores - top[..., None])
        sink_weight = jnp.exp(sink_column - top)
        total = jnp.sum(weights, -1) + sink_weight
        probs = weights / total[..., None]
        sink_prob = sink_weight / total
        probs_low = probs.astype(jnp.bfloat16)
        attended = jnp.einsum(
            "hgqk,hgkd->gqhd", probs_low, value_pick, preferred_element_type=jnp.float32
        )
        delta_rows = jnp.sum(grad_group.astype(jnp.float32) * attended, -1)
        delta = jnp.transpose(delta_rows, (2, 0, 1))
        dprobs = jnp.einsum(
            "gqhd,hgkd->hgqk", grad_group, value_pick, preferred_element_type=jnp.float32
        )
        dscores = (probs * (dprobs - delta[..., None])).astype(jnp.bfloat16)
        query_part = (
            jnp.einsum("hgqk,hgkd->gqhd", dscores, key_pick, preferred_element_type=jnp.float32)
            * scale
        ).astype(jnp.bfloat16)
        key_terms = (
            jnp.einsum("hgqk,gqhd->hgkd", dscores, query_group, preferred_element_type=jnp.float32)
            * scale
        )
        value_terms = jnp.einsum(
            "hgqk,gqhd->hgkd", probs_low, grad_group, preferred_element_type=jnp.float32
        )
        flat_table = table_group.reshape(-1)
        key_acc = key_acc.at[flat_table].add(
            key_terms.reshape(heads_here * group_blocks * KB, BLOCK, HEAD_DIM)
        )
        value_acc = value_acc.at[flat_table].add(
            value_terms.reshape(heads_here * group_blocks * KB, BLOCK, HEAD_DIM)
        )
        sink_acc = sink_acc - jnp.sum(sink_prob * delta, axis=(1, 2))
        return ((key_acc, value_acc, sink_acc), query_part)

    start = (
        jnp.zeros((blocks, BLOCK, HEAD_DIM), jnp.float32),
        jnp.zeros((blocks, BLOCK, HEAD_DIM), jnp.float32),
        jnp.zeros((heads_here,), jnp.float32),
    )
    finished, query_parts = lax.scan(advance, start, (query_steps, grad_steps, table_steps))
    key_acc, value_acc, sink_acc = finished
    query_local = query_parts.reshape(1, length, heads_here * HEAD_DIM)
    query_grad = lax.all_to_all(query_local, "seq", split_axis=1, concat_axis=2, tiled=True)
    kv_terms = jnp.stack(
        [key_acc.reshape(length, HEAD_DIM), value_acc.reshape(length, HEAD_DIM)], 0
    )
    returned = lax.all_to_all(kv_terms, "seq", split_axis=1, concat_axis=2, tiled=True)
    kv_back = returned.reshape(2, tokens_here, KV_HEADS, repeats, HEAD_DIM).sum(3)
    kv_back = kv_back.reshape(2, tokens_here, KV_HEADS * HEAD_DIM)
    key_grad = kv_back[0:1].astype(jnp.bfloat16)
    value_grad = kv_back[1:2].astype(jnp.bfloat16)
    sink_grad = lax.psum(sink_acc, "dp")
    return (query_grad, key_grad, value_grad, sink_grad)


F32 = jnp.float32
BF16 = jnp.bfloat16
GROUP = HEADS // KV_HEADS
SCALE = HEAD_DIM ** (-0.5)
LOG2E = 1.4426950408889634


def group_terms(keys, values, queries, grads, sink_row):
    nt = (((1,), (1,)), ((), ()))
    tn = (((0,), (0,)), ((), ()))
    scores = lax.dot_general(keys, queries, nt, preferred_element_type=F32)
    dprobs = lax.dot_general(values, grads, nt, preferred_element_type=F32)
    top = jnp.maximum(jnp.max(scores, 0, keepdims=True) * SCALE, sink_row)
    weights = jnp.exp2(scores * (SCALE * LOG2E) - top * LOG2E)
    sink_weight = jnp.exp(sink_row - top)
    inverse = 1.0 / (jnp.sum(weights, 0, keepdims=True) + sink_weight)
    probs = weights * inverse
    probs_low = probs.astype(BF16)
    delta = jnp.sum(probs_low.astype(F32) * dprobs, 0, keepdims=True)
    dscores = (probs * (dprobs - delta)).astype(BF16)
    value_terms = jnp.dot(probs_low, grads, preferred_element_type=F32)
    key_terms = jnp.dot(dscores, queries, preferred_element_type=F32)
    query_terms = lax.dot_general(keys, dscores, tn, preferred_element_type=F32)
    return key_terms, value_terms, query_terms.T * SCALE, -(sink_weight * inverse) * delta


def dense_kernel(
    q_ref, g_ref, k_ref, v_ref, sink_ref,
    dq_ref, dk_ref, dv_ref, ds_ref,
    kv_all, acc, part, pair_out, pair_in, right_out, right_in, left_out, left_in,
    sink_all, sink_part, sink_in, sink_dp, q_here, g_here, dq_here, dk_here, dv_here,
    right_s, right_r, left_s, left_r, sib_s, sib_r, pair_s, pair_r,
    sumr_s, sumr_r, suml_s, suml_r, logit_s, logit_r, sg_s, sg_r, dp_s, dp_r, load_s, rows_s, leave_s,
):
    devices = lax.axis_size("seq")
    chips = devices // 2
    last = chips - 1
    dps = lax.axis_size("dp")
    me = lax.axis_index("seq")
    my_dp = lax.axis_index("dp")
    chip = lax.div(me, 2)
    lane = lax.rem(me, 2)
    sibling = me + 1 - 2 * lane
    here = HEAD_DIM
    wide = GROUP * HEAD_DIM

    def remote(src, dst, send_sem, recv_sem, **target):
        return pltpu.make_async_remote_copy(
            src_ref=src, dst_ref=dst, send_sem=send_sem, recv_sem=recv_sem,
            device_id=target, device_id_type=pl.DeviceIdType.MESH,
        )

    def shard(h, z, which):
        return kv_all.at[:, h, 2 * z + which]

    def go_right(h, k, z):
        ref = shard(h, z, lane)
        return remote(ref, ref, right_s.at[h, k], right_r.at[h, k], seq=me + 2)

    def go_left(h, k, z):
        ref = shard(h, z, lane)
        return remote(ref, ref, left_s.at[h, k], left_r.at[h, k], seq=me - 2)

    def go_across(h, z, which):
        ref = shard(h, z, which)
        return remote(ref, ref, sib_s.at[h, z], sib_r.at[h, z], seq=sibling)

    def go_pair(h):
        return remote(pair_out.at[h], pair_in.at[h], pair_s.at[h], pair_r.at[h], seq=sibling)

    def sum_right(h, d):
        return remote(
            right_out.at[h, d], right_in.at[h, d], sumr_s.at[h, d], sumr_r.at[h, d], seq=me + 2
        )

    def sum_left(h, d):
        return remote(
            left_out.at[h, d], left_in.at[h, d], suml_s.at[h, d], suml_r.at[h, d], seq=me - 2
        )

    def logit(i, owner):
        ref = sink_all.at[owner]
        return remote(ref, ref, logit_s.at[i], logit_r.at[i], seq=lax.rem(me + i, devices))

    def sink_send(h):
        return remote(sink_part.at[h], sink_in.at[me], sg_s.at[h], sg_r.at[me], seq=h)

    def sink_recv(p):
        return remote(sink_part.at[p], sink_in.at[p], sg_s.at[p], sg_r.at[p], seq=p)

    def across_dp(i, owner):
        ref = sink_dp.at[owner]
        return remote(ref, ref, dp_s.at[i], dp_r.at[i], dp=lax.rem(my_dp + i, dps))

    barrier = pltpu.get_barrier_semaphore()
    for i in range(1, devices):
        pl.semaphore_signal(
            barrier, inc=1, device_id={"seq": lax.rem(me + i, devices)},
            device_id_type=pl.DeviceIdType.MESH,
        )
    for i in range(1, dps):
        pl.semaphore_signal(
            barrier, inc=1, device_id={"dp": lax.rem(my_dp + i, dps)},
            device_id_type=pl.DeviceIdType.MESH,
        )

    def load(which, h):
        ref = (k_ref, v_ref)[which]
        cut = pl.ds(pl.multiple_of(h * HEAD_DIM, HEAD_DIM), HEAD_DIM)
        return pltpu.make_async_copy(ref.at[:, cut], kv_all.at[which, h, me], load_s.at[which, h])

    rows = (
        pltpu.make_async_copy(q_ref, q_here, rows_s.at[0]),
        pltpu.make_async_copy(g_ref, g_here, rows_s.at[1]),
    )
    for h in range(KV_HEADS):
        for which in range(2):
            load(which, h).start()
    for copy in rows:
        copy.start()
    sink_all[me] = jnp.zeros_like(sink_all[me])
    for j in range(GROUP):
        sink_all[me, j : j + 1, :] = jnp.full((1, HEAD_DIM), sink_ref[j], F32)
    sink_part[...] = jnp.zeros_like(sink_part)
    pl.semaphore_wait(barrier, devices - 1 + dps - 1)

    def leave(which, h):
        held, out = ((dq_here, dq_ref), (dk_here, dk_ref), (dv_here, dv_ref))[which]
        size = wide if which == 0 else HEAD_DIM
        cut = pl.ds(pl.multiple_of(h * size, size), size)
        return pltpu.make_async_copy(held.at[:, cut], out.at[:, cut], leave_s.at[which, h])

    def send_own(h):
        for which in range(2):
            load(which, h).wait()

        @pl.when(chip < last)
        def _():
            go_right(h, 0, chip).start()

        @pl.when(chip > 0)
        def _():
            go_left(h, 0, chip).start()

        go_across(h, chip, lane).start()

    send_own(0)
    for i in range(1, devices):
        logit(i, me).start()

    def ready_to_compute():
        for copy in rows:
            copy.wait()
        for i in range(1, devices):
            logit(i, lax.rem(me - i + devices, devices)).wait_recv()

    def hand_on(h, k):
        @pl.when(chip >= k)
        def _():
            go_right(h, k - 1, chip - k).wait_recv()
            if k < last:

                @pl.when(chip < last)
                def _():
                    go_right(h, k, chip - k).start()

            go_across(h, chip - k, lane).start()

        @pl.when(chip + k <= last)
        def _():
            go_left(h, k - 1, chip + k).wait_recv()
            if k < last:

                @pl.when(chip > 0)
                def _():
                    go_left(h, k, chip + k).start()

            go_across(h, chip + k, lane).start()

    def compute(h):
        for z in range(chips):
            go_across(h, z, 1 - lane).wait_recv()
        keys = kv_all[0, h].reshape(devices * here, HEAD_DIM)
        values = kv_all[1, h].reshape(devices * here, HEAD_DIM)
        key_sum = value_sum = None
        for half in range(2):
            heads = range(half * GROUP // 2, (half + 1) * GROUP // 2)
            cuts = [pl.ds(pl.multiple_of(h * wide + j * HEAD_DIM, HEAD_DIM), HEAD_DIM) for j in heads]
            queries = jnp.concatenate([q_here[:, cut] for cut in cuts], 0)
            grads = jnp.concatenate([g_here[:, cut] for cut in cuts], 0)
            sink_row = jnp.concatenate([sink_all[h, j : j + 1, :] for j in heads], 1)
            key_terms, value_terms, query_terms, sink_terms = group_terms(
                keys, values, queries, grads, sink_row
            )
            for i, j in enumerate(heads):
                span = slice(i * here, (i + 1) * here)
                dq_here[:, cuts[i]] = query_terms[span].astype(BF16)
                sink_part[h, j : j + 1, :] = sink_terms[:, span]
            key_sum = key_terms if half == 0 else key_sum + key_terms
            value_sum = value_terms if half == 0 else value_sum + value_terms
        acc[0] = (key_sum * SCALE).reshape(devices, here, HEAD_DIM)
        acc[1] = value_sum.reshape(devices, here, HEAD_DIM)
        for d in range(chips):
            pair_out[h, d] = acc[:, 2 * d + 1 - lane].astype(BF16)
        go_pair(h).start()
        leave(0, h).start()
        for d in range(chips):
            part[h, d] = acc[:, 2 * d + lane]

        @pl.when(h == me)
        def _():
            sink_in[me] = sink_part[h]

        @pl.when(h != me)
        def _():
            sink_send(h).start()

    def pair_sum(h):
        go_pair(h).wait_recv()
        for d in range(chips):
            part[h, d] = part[h, d] + pair_in[h, d].astype(F32)

    def pass_right(h):
        for d in range(last, 0, -1):

            @pl.when(d > chip)
            def _():
                @pl.when(chip == 0)
                def _():
                    right_out[h, d] = part[h, d].astype(BF16)

                @pl.when(chip > 0)
                def _():
                    sum_right(h, d).wait_recv()
                    right_out[h, d] = (part[h, d] + right_in[h, d].astype(F32)).astype(BF16)

                sum_right(h, d).start()

    def pass_left(h):
        for d in range(last):

            @pl.when(d < chip)
            def _():
                @pl.when(chip == last)
                def _():
                    left_out[h, d] = part[h, d].astype(BF16)

                @pl.when(chip < last)
                def _():
                    sum_left(h, d).wait_recv()
                    left_out[h, d] = (part[h, d] + left_in[h, d].astype(F32)).astype(BF16)

                sum_left(h, d).start()

    def finish(h):
        @pl.when(chip > 0)
        def _():
            sum_right(h, chip).wait_recv()
            part[h, chip] = part[h, chip] + right_in[h, chip].astype(F32)

        @pl.when(chip < last)
        def _():
            sum_left(h, chip).wait_recv()
            part[h, chip] = part[h, chip] + left_in[h, chip].astype(F32)

        cut = pl.ds(pl.multiple_of(h * HEAD_DIM, HEAD_DIM), HEAD_DIM)
        dk_here[:, cut] = part[h, chip, 0].astype(BF16)
        dv_here[:, cut] = part[h, chip, 1].astype(BF16)
        leave(1, h).start()
        leave(2, h).start()

    def sink_sum():
        for p in range(devices):

            @pl.when(p != me)
            def _():
                sink_recv(p).wait_recv()

        sink_dp[my_dp] = jnp.sum(sink_in[...], 0)
        for i in range(1, dps):
            across_dp(i, my_dp).start()

    def in_range(h):
        return (h >= 0) & (h < KV_HEADS)

    compute_at = chips
    pair_at = compute_at + 1
    finish_at = pair_at + 2 * last - 1

    def tick(t, carry):
        def at(h, step, also=None):
            ready = in_range(h) if also is None else in_range(h) & also

            @pl.when(ready)
            def _():
                step(h)

        pl.when(t == compute_at)(ready_to_compute)
        at(t - compute_at, compute)
        at(t - pair_at, pair_sum)
        at(t - 3, lambda h: hand_on(h, 3))
        at(t - pair_at - chip, pass_right, chip < last)
        at(t - pair_at - (last - chip), pass_left, chip > 0)
        at(t - 2, lambda h: hand_on(h, 2))
        at(t - 1, lambda h: hand_on(h, 1))
        at(t + 1, send_own)
        at(t - finish_at, finish)
        pl.when(t == compute_at + KV_HEADS + 1)(sink_sum)
        return carry

    lax.fori_loop(0, finish_at + KV_HEADS, tick, 0)

    for i in range(1, dps):
        across_dp(i, lax.rem(my_dp - i + dps, dps)).wait_recv()
    total = sink_dp[0]
    for i in range(1, dps):
        total = total + sink_dp[i]
    for j in range(GROUP):
        ds_ref[j] = jnp.sum(total[j : j + 1])

    def drain(h, carry):
        for k in range(last):

            @pl.when((chip >= k) & (chip < last))
            def _():
                go_right(h, k, chip - k).wait_send()

            @pl.when((chip + k <= last) & (chip > 0))
            def _():
                go_left(h, k, chip + k).wait_send()

        for z in range(chips):
            go_across(h, z, lane).wait_send()
        go_pair(h).wait_send()
        for which in range(3):
            leave(which, h).wait()
        for d in range(chips):

            @pl.when(d > chip)
            def _():
                sum_right(h, d).wait_send()

            @pl.when(d < chip)
            def _():
                sum_left(h, d).wait_send()

        @pl.when(h != me)
        def _():
            sink_send(h).wait_send()

        return carry

    lax.fori_loop(0, KV_HEADS, drain, 0)
    for i in range(1, devices):
        logit(i, me).wait_send()
    for i in range(1, dps):
        across_dp(i, my_dp).wait_send()


def place_kernel(*refs):
    held, out, sems = refs[:4], refs[4:8], refs[8]
    copies = [pltpu.make_async_copy(held[i], out[i], sems.at[i]) for i in range(3)]
    for copy in copies:
        copy.start()
    for j in range(GROUP):
        out[3][j] = held[3][j]
    for copy in copies:
        copy.wait()


def dense_shards(queries, key_states, value_states, sink_logit, out_grad, block_table):
    devices = lax.axis_size("seq")
    chips = devices // 2
    dps = lax.axis_size("dp")
    here = queries.shape[1]
    tile = (here, HEAD_DIM)
    dma = pltpu.SemaphoreType.DMA
    hbm = pl.BlockSpec(memory_space=pltpu.HBM)
    smem = pl.BlockSpec(memory_space=pltpu.SMEM)
    flat = KV_HEADS * HEAD_DIM
    steps = [(KV_HEADS, chips - 1)] * 4 + [(KV_HEADS, chips)] * 2 + [(KV_HEADS,)] * 2
    steps += [(KV_HEADS, chips)] * 4 + [(devices,)] * 4 + [(dps,)] * 2 + [(2, KV_HEADS), (2,), (3, KV_HEADS)]
    per_head = pltpu.VMEM((KV_HEADS, chips, 2) + tile, BF16)
    results = [
        jax.ShapeDtypeStruct((here, HEADS * HEAD_DIM), BF16),
        jax.ShapeDtypeStruct((here, flat), BF16),
        jax.ShapeDtypeStruct((here, flat), BF16),
        jax.ShapeDtypeStruct((GROUP,), F32),
    ]
    held = pl.pallas_call(
        dense_kernel,
        in_specs=[hbm] * 4 + [smem],
        out_specs=[hbm] * 3 + [smem],
        out_shape=results,
        scratch_shapes=[
            pltpu.VMEM((2, KV_HEADS, devices) + tile, BF16),
            pltpu.VMEM((2, devices) + tile, F32),
            pltpu.VMEM((KV_HEADS, chips, 2) + tile, F32),
        ]
        + [per_head] * 6
        + [
            pltpu.VMEM((devices, 8, HEAD_DIM), F32),
            pltpu.VMEM((KV_HEADS, 8, HEAD_DIM), F32),
            pltpu.VMEM((devices, 8, HEAD_DIM), F32),
            pltpu.VMEM((dps, 8, HEAD_DIM), F32),
        ]
        + [pltpu.VMEM((here, HEADS * HEAD_DIM), BF16)] * 3
        + [pltpu.VMEM((here, flat), BF16)] * 2
        + [dma(step) for step in steps],
        compiler_params=pltpu.CompilerParams(
            collective_id=0, has_side_effects=True, vmem_limit_bytes=62 * 2**20
        ),
    )(queries[0], out_grad[0], key_states[0], value_states[0], sink_logit)
    query_grad, key_grad, value_grad, sink_grad = pl.pallas_call(
        place_kernel,
        in_specs=[pl.BlockSpec(memory_space=pltpu.VMEM)] * 3 + [smem],
        out_specs=[hbm] * 3 + [smem],
        out_shape=results,
        scratch_shapes=[dma((3,))],
        compiler_params=pltpu.CompilerParams(vmem_limit_bytes=62 * 2**20),
    )(*held)
    return query_grad[None], key_grad[None], value_grad[None], sink_grad


def shards(queries, key_states, value_states, sink_logit, out_grad, block_table):
    devices = lax.axis_size("seq")
    dense = queries.shape[1] == BLOCK and devices == KB and devices == KV_HEADS
    part = dense_shards if dense else sparse_shards
    return part(queries, key_states, value_states, sink_logit, out_grad, block_table)


def solution(mesh):
    in_specs = (
        P("dp", "seq", None),
        P("dp", "seq", None),
        P("dp", "seq", None),
        P("seq"),
        P("dp", "seq", None),
        P("seq", None, None),
    )
    out_specs = (P("dp", "seq", None), P("dp", "seq", None), P("dp", "seq", None), P("seq"))
    return jax.shard_map(shards, mesh=mesh, in_specs=in_specs, out_specs=out_specs, check_vma=False)
```

```python
import functools

import jax
import jax.numpy as jnp
from jax import lax
from jax.experimental import pallas as pl
from jax.experimental.pallas import tpu as pltpu
from jax.sharding import PartitionSpec as P

HEADS = 32
KV_HEADS = 8
HEAD_DIM = 128
BLOCK = 128
KB = 8


def sparse_shards(queries, key_states, value_states, sink_logit, out_grad, block_table):
    devices = lax.axis_size("seq")
    tokens_here = queries.shape[1]
    length = tokens_here * devices
    heads_here = HEADS // devices
    group = HEADS // KV_HEADS
    repeats = devices // KV_HEADS
    blocks = length // BLOCK
    scale = HEAD_DIM ** (-0.5)
    key_wide = jnp.repeat(key_states.reshape(1, tokens_here, KV_HEADS, 1, HEAD_DIM), group, axis=3)
    key_wide = key_wide.reshape(1, tokens_here, HEADS * HEAD_DIM)
    value_wide = jnp.repeat(
        value_states.reshape(1, tokens_here, KV_HEADS, 1, HEAD_DIM), group, axis=3
    )
    value_wide = value_wide.reshape(1, tokens_here, HEADS * HEAD_DIM)
    query_all, grad_all, key_all, value_all = (
        lax.all_to_all(queries, "seq", split_axis=2, concat_axis=1, tiled=True),
        lax.all_to_all(out_grad, "seq", split_axis=2, concat_axis=1, tiled=True),
        lax.all_to_all(key_wide, "seq", split_axis=2, concat_axis=1, tiled=True),
        lax.all_to_all(value_wide, "seq", split_axis=2, concat_axis=1, tiled=True),
    )
    key_rows = key_all[0, :, :HEAD_DIM]
    value_rows = value_all[0, :, :HEAD_DIM]
    group_blocks = max(4, blocks // 8)
    step_count = blocks // group_blocks
    query_steps = query_all.reshape(step_count, group_blocks, BLOCK, heads_here, HEAD_DIM)
    grad_steps = grad_all.reshape(step_count, group_blocks, BLOCK, heads_here, HEAD_DIM)
    table_steps = block_table.reshape(heads_here, step_count, group_blocks, KB).transpose(
        1, 0, 2, 3
    )
    key_table = key_rows.reshape(blocks, BLOCK, HEAD_DIM)
    value_table = value_rows.reshape(blocks, BLOCK, HEAD_DIM)
    sink_column = sink_logit[:, None, None]

    def advance(carry, items):
        key_acc, value_acc, sink_acc = carry
        query_group, grad_group, table_group = items
        key_pick = key_table[table_group].reshape(heads_here, group_blocks, KB * BLOCK, HEAD_DIM)
        value_pick = value_table[table_group].reshape(
            heads_here, group_blocks, KB * BLOCK, HEAD_DIM
        )
        scores = (
            jnp.einsum("gqhd,hgkd->hgqk", query_group, key_pick, preferred_element_type=jnp.float32)
            * scale
        )
        top = jnp.maximum(jnp.max(scores, -1), sink_column)
        weights = jnp.exp(scores - top[..., None])
        sink_weight = jnp.exp(sink_column - top)
        total = jnp.sum(weights, -1) + sink_weight
        probs = weights / total[..., None]
        sink_prob = sink_weight / total
        probs_low = probs.astype(jnp.bfloat16)
        attended = jnp.einsum(
            "hgqk,hgkd->gqhd", probs_low, value_pick, preferred_element_type=jnp.float32
        )
        delta_rows = jnp.sum(grad_group.astype(jnp.float32) * attended, -1)
        delta = jnp.transpose(delta_rows, (2, 0, 1))
        dprobs = jnp.einsum(
            "gqhd,hgkd->hgqk", grad_group, value_pick, preferred_element_type=jnp.float32
        )
        dscores = (probs * (dprobs - delta[..., None])).astype(jnp.bfloat16)
        query_part = (
            jnp.einsum("hgqk,hgkd->gqhd", dscores, key_pick, preferred_element_type=jnp.float32)
            * scale
        ).astype(jnp.bfloat16)
        key_terms = (
            jnp.einsum("hgqk,gqhd->hgkd", dscores, query_group, preferred_element_type=jnp.float32)
            * scale
        )
        value_terms = jnp.einsum(
            "hgqk,gqhd->hgkd", probs_low, grad_group, preferred_element_type=jnp.float32
        )
        flat_table = table_group.reshape(-1)
        key_acc = key_acc.at[flat_table].add(
            key_terms.reshape(heads_here * group_blocks * KB, BLOCK, HEAD_DIM)
        )
        value_acc = value_acc.at[flat_table].add(
            value_terms.reshape(heads_here * group_blocks * KB, BLOCK, HEAD_DIM)
        )
        sink_acc = sink_acc - jnp.sum(sink_prob * delta, axis=(1, 2))
        return ((key_acc, value_acc, sink_acc), query_part)

    start = (
        jnp.zeros((blocks, BLOCK, HEAD_DIM), jnp.float32),
        jnp.zeros((blocks, BLOCK, HEAD_DIM), jnp.float32),
        jnp.zeros((heads_here,), jnp.float32),
    )
    finished, query_parts = lax.scan(advance, start, (query_steps, grad_steps, table_steps))
    key_acc, value_acc, sink_acc = finished
    query_local = query_parts.reshape(1, length, heads_here * HEAD_DIM)
    query_grad = lax.all_to_all(query_local, "seq", split_axis=1, concat_axis=2, tiled=True)
    kv_terms = jnp.stack(
        [key_acc.reshape(length, HEAD_DIM), value_acc.reshape(length, HEAD_DIM)], 0
    )
    returned = lax.all_to_all(kv_terms, "seq", split_axis=1, concat_axis=2, tiled=True)
    kv_back = returned.reshape(2, tokens_here, KV_HEADS, repeats, HEAD_DIM).sum(3)
    kv_back = kv_back.reshape(2, tokens_here, KV_HEADS * HEAD_DIM)
    key_grad = kv_back[0:1].astype(jnp.bfloat16)
    value_grad = kv_back[1:2].astype(jnp.bfloat16)
    sink_grad = lax.psum(sink_acc, "dp")
    return (query_grad, key_grad, value_grad, sink_grad)


F32 = jnp.float32
BF16 = jnp.bfloat16
GROUP = HEADS // KV_HEADS
SCALE = HEAD_DIM ** (-0.5)
AHEAD = 4
LOG2E = 1.4426950408889634


def group_terms(keys, values, queries, grads, sink_row):
    nt = (((1,), (1,)), ((), ()))
    tn = (((0,), (0,)), ((), ()))
    scores = lax.dot_general(keys, queries, nt, preferred_element_type=F32)
    dprobs = lax.dot_general(values, grads, nt, preferred_element_type=F32)
    top = jnp.maximum(jnp.max(scores, 0, keepdims=True) * SCALE, sink_row)
    weights = jnp.exp2(scores * (SCALE * LOG2E) - top * LOG2E)
    sink_weight = jnp.exp(sink_row - top)
    inverse = 1.0 / (jnp.sum(weights, 0, keepdims=True) + sink_weight)
    probs = weights * inverse
    probs_low = probs.astype(BF16)
    delta = jnp.sum(probs_low.astype(F32) * dprobs, 0, keepdims=True)
    dscores = (probs * (dprobs - delta)).astype(BF16)
    value_terms = jnp.dot(probs_low, grads, preferred_element_type=F32)
    key_terms = jnp.dot(dscores, queries, preferred_element_type=F32)
    query_terms = lax.dot_general(keys, dscores, tn, preferred_element_type=F32)
    return key_terms, value_terms, query_terms.T * SCALE, -(sink_weight * inverse) * delta


def dense_kernel(
    q_ref, g_ref, k_ref, v_ref, sink_ref,
    dq_ref, dk_ref, dv_ref, ds_ref,
    kv_all, acc, part, pair_out, pair_in, right_out, right_in, left_out, left_in,
    sink_all, sink_part, sink_in, sink_dp, q_here, g_here, dq_here, dk_here, dv_here,
    right_s, right_r, left_s, left_r, sib_s, sib_r, pair_s, pair_r,
    sumr_s, sumr_r, suml_s, suml_r, logit_s, logit_r, sg_s, sg_r, dp_s, dp_r, load_s, rows_s, leave_s,
):
    devices = lax.axis_size("seq")
    chips = devices // 2
    last = chips - 1
    dps = lax.axis_size("dp")
    me = lax.axis_index("seq")
    my_dp = lax.axis_index("dp")
    chip = lax.div(me, 2)
    lane = lax.rem(me, 2)
    sibling = me + 1 - 2 * lane
    here = HEAD_DIM
    wide = GROUP * HEAD_DIM

    def remote(src, dst, send_sem, recv_sem, **target):
        return pltpu.make_async_remote_copy(
            src_ref=src, dst_ref=dst, send_sem=send_sem, recv_sem=recv_sem,
            device_id=target, device_id_type=pl.DeviceIdType.MESH,
        )

    def shard(h, z, which):
        return kv_all.at[:, h, 2 * z + which]

    def go_right(h, k, z):
        ref = shard(h, z, lane)
        return remote(ref, ref, right_s.at[h, k], right_r.at[h, k], seq=me + 2)

    def go_left(h, k, z):
        ref = shard(h, z, lane)
        return remote(ref, ref, left_s.at[h, k], left_r.at[h, k], seq=me - 2)

    def go_across(h, z, which):
        ref = shard(h, z, which)
        return remote(ref, ref, sib_s.at[h, z], sib_r.at[h, z], seq=sibling)

    def go_pair(h):
        return remote(pair_out.at[h], pair_in.at[h], pair_s.at[h], pair_r.at[h], seq=sibling)

    def sum_right(h, d):
        return remote(
            right_out.at[h, d], right_in.at[h, d], sumr_s.at[h, d], sumr_r.at[h, d], seq=me + 2
        )

    def sum_left(h, d):
        return remote(
            left_out.at[h, d], left_in.at[h, d], suml_s.at[h, d], suml_r.at[h, d], seq=me - 2
        )

    def logit(i, owner):
        ref = sink_all.at[owner]
        return remote(ref, ref, logit_s.at[i], logit_r.at[i], seq=lax.rem(me + i, devices))

    def sink_send(h):
        return remote(sink_part.at[h], sink_in.at[me], sg_s.at[h], sg_r.at[me], seq=h)

    def sink_recv(p):
        return remote(sink_part.at[p], sink_in.at[p], sg_s.at[p], sg_r.at[p], seq=p)

    def across_dp(i, owner):
        ref = sink_dp.at[owner]
        return remote(ref, ref, dp_s.at[i], dp_r.at[i], dp=lax.rem(my_dp + i, dps))

    barrier = pltpu.get_barrier_semaphore()
    for i in range(1, devices):
        pl.semaphore_signal(
            barrier, inc=1, device_id={"seq": lax.rem(me + i, devices)},
            device_id_type=pl.DeviceIdType.MESH,
        )
    for i in range(1, dps):
        pl.semaphore_signal(
            barrier, inc=1, device_id={"dp": lax.rem(my_dp + i, dps)},
            device_id_type=pl.DeviceIdType.MESH,
        )

    def load(which, h):
        ref = (k_ref, v_ref)[which]
        cut = pl.ds(pl.multiple_of(h * HEAD_DIM, HEAD_DIM), HEAD_DIM)
        return pltpu.make_async_copy(ref.at[:, cut], kv_all.at[which, h, me], load_s.at[which, h])

    rows = (
        pltpu.make_async_copy(q_ref, q_here, rows_s.at[0]),
        pltpu.make_async_copy(g_ref, g_here, rows_s.at[1]),
    )
    for h in range(KV_HEADS):
        for which in range(2):
            load(which, h).start()
    for copy in rows:
        copy.start()
    sink_all[me] = jnp.zeros_like(sink_all[me])
    for j in range(GROUP):
        sink_all[me, j : j + 1, :] = jnp.full((1, HEAD_DIM), sink_ref[j], F32)
    sink_part[...] = jnp.zeros_like(sink_part)
    pl.semaphore_wait(barrier, devices - 1 + dps - 1)

    def leave(which, h):
        held, out = ((dq_here, dq_ref), (dk_here, dk_ref), (dv_here, dv_ref))[which]
        size = wide if which == 0 else HEAD_DIM
        cut = pl.ds(pl.multiple_of(h * size, size), size)
        return pltpu.make_async_copy(held.at[:, cut], out.at[:, cut], leave_s.at[which, h])

    def send_right(h):
        go_right(h, 0, chip).start()

    def send_left(h):
        go_left(h, 0, chip).start()

    def send_across(h):
        go_across(h, chip, lane).start()

    far = last - chip
    right_ahead = 1 + AHEAD * (1 - jnp.minimum(chip, 1))
    left_ahead = 1 + AHEAD * (1 - jnp.minimum(far, 1))
    for h in range(KV_HEADS):
        for which in range(2):
            load(which, h).wait()
    send_across(0)
    for h in range(AHEAD + 1):
        pl.when((chip < last) & (h < right_ahead))(functools.partial(send_right, h))
        pl.when((chip > 0) & (h < left_ahead))(functools.partial(send_left, h))
    for i in range(1, devices):
        logit(i, me).start()

    def ready_to_compute():
        for copy in rows:
            copy.wait()
        for i in range(1, devices):
            logit(i, lax.rem(me - i + devices, devices)).wait_recv()

    def hand_on(h, k):
        @pl.when(chip >= k)
        def _():
            go_right(h, k - 1, chip - k).wait_recv()
            if k < last:

                @pl.when(chip < last)
                def _():
                    go_right(h, k, chip - k).start()

            go_across(h, chip - k, lane).start()

        @pl.when(chip + k <= last)
        def _():
            go_left(h, k - 1, chip + k).wait_recv()
            if k < last:

                @pl.when(chip > 0)
                def _():
                    go_left(h, k, chip + k).start()

            go_across(h, chip + k, lane).start()

    def compute(h):
        for z in range(chips):
            go_across(h, z, 1 - lane).wait_recv()
        keys = kv_all[0, h].reshape(devices * here, HEAD_DIM)
        values = kv_all[1, h].reshape(devices * here, HEAD_DIM)
        key_sum = value_sum = None
        for half in range(2):
            heads = range(half * GROUP // 2, (half + 1) * GROUP // 2)
            cuts = [pl.ds(pl.multiple_of(h * wide + j * HEAD_DIM, HEAD_DIM), HEAD_DIM) for j in heads]
            queries = jnp.concatenate([q_here[:, cut] for cut in cuts], 0)
            grads = jnp.concatenate([g_here[:, cut] for cut in cuts], 0)
            sink_row = jnp.concatenate([sink_all[h, j : j + 1, :] for j in heads], 1)
            key_terms, value_terms, query_terms, sink_terms = group_terms(
                keys, values, queries, grads, sink_row
            )
            for i, j in enumerate(heads):
                span = slice(i * here, (i + 1) * here)
                dq_here[:, cuts[i]] = query_terms[span].astype(BF16)
                sink_part[h, j : j + 1, :] = sink_terms[:, span]
            key_sum = key_terms if half == 0 else key_sum + key_terms
            value_sum = value_terms if half == 0 else value_sum + value_terms
        acc[0] = (key_sum * SCALE).reshape(devices, here, HEAD_DIM)
        acc[1] = value_sum.reshape(devices, here, HEAD_DIM)
        for d in range(chips):
            pair_out[h, d] = acc[:, 2 * d + 1 - lane].astype(BF16)
        go_pair(h).start()
        leave(0, h).start()
        for d in range(chips):
            part[h, d] = acc[:, 2 * d + lane]

        @pl.when(h == me)
        def _():
            sink_in[me] = sink_part[h]

        @pl.when(h != me)
        def _():
            sink_send(h).start()

    def pair_sum(h):
        go_pair(h).wait_recv()
        for d in range(chips):
            part[h, d] = part[h, d] + pair_in[h, d].astype(F32)

    def pass_right(h):
        for d in range(last, 0, -1):

            @pl.when(d > chip)
            def _():
                @pl.when(chip == 0)
                def _():
                    right_out[h, d] = part[h, d].astype(BF16)

                @pl.when(chip > 0)
                def _():
                    sum_right(h, d).wait_recv()
                    right_out[h, d] = (part[h, d] + right_in[h, d].astype(F32)).astype(BF16)

                sum_right(h, d).start()

    def pass_left(h):
        for d in range(last):

            @pl.when(d < chip)
            def _():
                @pl.when(chip == last)
                def _():
                    left_out[h, d] = part[h, d].astype(BF16)

                @pl.when(chip < last)
                def _():
                    sum_left(h, d).wait_recv()
                    left_out[h, d] = (part[h, d] + left_in[h, d].astype(F32)).astype(BF16)

                sum_left(h, d).start()

    def finish(h):
        @pl.when(chip > 0)
        def _():
            sum_right(h, chip).wait_recv()
            part[h, chip] = part[h, chip] + right_in[h, chip].astype(F32)

        @pl.when(chip < last)
        def _():
            sum_left(h, chip).wait_recv()
            part[h, chip] = part[h, chip] + left_in[h, chip].astype(F32)

        cut = pl.ds(pl.multiple_of(h * HEAD_DIM, HEAD_DIM), HEAD_DIM)
        dk_here[:, cut] = part[h, chip, 0].astype(BF16)
        dv_here[:, cut] = part[h, chip, 1].astype(BF16)
        leave(1, h).start()
        leave(2, h).start()

    def sink_sum():
        for p in range(devices):

            @pl.when(p != me)
            def _():
                sink_recv(p).wait_recv()

        sink_dp[my_dp] = jnp.sum(sink_in[...], 0)
        for i in range(1, dps):
            across_dp(i, my_dp).start()

    def in_range(h):
        return (h >= 0) & (h < KV_HEADS)

    compute_at = chips
    pair_at = compute_at + 1
    finish_at = pair_at + 2 * last + 2

    def tick(t, carry):
        def at(h, step, also=None):
            ready = in_range(h) if also is None else in_range(h) & also

            @pl.when(ready)
            def _():
                step(h)

        pl.when(t == compute_at)(ready_to_compute)
        at(t - finish_at, finish)
        at(t - compute_at, compute)
        at(t - pair_at, pair_sum)
        at(t - 3, lambda h: hand_on(h, 3))
        at(t - pair_at - far - jnp.minimum(far, 1), pass_left, chip > 0)
        at(t - pair_at - chip - jnp.minimum(chip, 1), pass_right, chip < last)
        at(t - 2, lambda h: hand_on(h, 2))
        at(t - 1, lambda h: hand_on(h, 1))
        at(t + right_ahead, send_right, chip < last)
        at(t + left_ahead, send_left, chip > 0)
        at(t + 1, send_across)
        pl.when(t == compute_at + KV_HEADS + 1)(sink_sum)
        return carry

    lax.fori_loop(0, finish_at + KV_HEADS, tick, 0)

    for i in range(1, dps):
        across_dp(i, lax.rem(my_dp - i + dps, dps)).wait_recv()
    total = sink_dp[0]
    for i in range(1, dps):
        total = total + sink_dp[i]
    for j in range(GROUP):
        ds_ref[j] = jnp.sum(total[j : j + 1])

    def drain(h, carry):
        for k in range(last):

            @pl.when((chip >= k) & (chip < last))
            def _():
                go_right(h, k, chip - k).wait_send()

            @pl.when((chip + k <= last) & (chip > 0))
            def _():
                go_left(h, k, chip + k).wait_send()

        for z in range(chips):
            go_across(h, z, lane).wait_send()
        go_pair(h).wait_send()
        for which in range(3):
            leave(which, h).wait()
        for d in range(chips):

            @pl.when(d > chip)
            def _():
                sum_right(h, d).wait_send()

            @pl.when(d < chip)
            def _():
                sum_left(h, d).wait_send()

        @pl.when(h != me)
        def _():
            sink_send(h).wait_send()

        return carry

    lax.fori_loop(0, KV_HEADS, drain, 0)
    for i in range(1, devices):
        logit(i, me).wait_send()
    for i in range(1, dps):
        across_dp(i, my_dp).wait_send()


def place_kernel(*refs):
    held, out, space, come, go = refs[:4], refs[4:8], refs[8:11], refs[11], refs[12]
    rows = held[0].shape[0] // 4
    cuts = [(0, pl.ds(i * rows, rows)) for i in range(4)]
    cuts += [(1, pl.ds(0, 4 * rows)), (2, pl.ds(0, 4 * rows))]
    loads, stores = [], []
    for i, (which, cut) in enumerate(cuts):
        here = space[which].at[cut]
        loads.append(pltpu.make_async_copy(held[which].at[cut], here, come.at[i]))
        stores.append(pltpu.make_async_copy(here, out[which].at[cut], go.at[i]))
    for copy in loads:
        copy.start()
    for j in range(GROUP):
        out[3][j] = held[3][j]
    for first, second in zip(loads, stores):
        first.wait()
        second.start()
    for copy in stores:
        copy.wait()


def dense_shards(queries, key_states, value_states, sink_logit, out_grad, block_table):
    devices = lax.axis_size("seq")
    chips = devices // 2
    dps = lax.axis_size("dp")
    here = queries.shape[1]
    tile = (here, HEAD_DIM)
    dma = pltpu.SemaphoreType.DMA
    hbm = pl.BlockSpec(memory_space=pltpu.HBM)
    smem = pl.BlockSpec(memory_space=pltpu.SMEM)
    flat = KV_HEADS * HEAD_DIM
    steps = [(KV_HEADS, chips - 1)] * 4 + [(KV_HEADS, chips)] * 2 + [(KV_HEADS,)] * 2
    steps += [(KV_HEADS, chips)] * 4 + [(devices,)] * 4 + [(dps,)] * 2 + [(2, KV_HEADS), (2,), (3, KV_HEADS)]
    per_head = pltpu.VMEM((KV_HEADS, chips, 2) + tile, BF16)
    results = [
        jax.ShapeDtypeStruct((here, HEADS * HEAD_DIM), BF16),
        jax.ShapeDtypeStruct((here, flat), BF16),
        jax.ShapeDtypeStruct((here, flat), BF16),
        jax.ShapeDtypeStruct((GROUP,), F32),
    ]
    held = pl.pallas_call(
        dense_kernel,
        in_specs=[hbm] * 4 + [smem],
        out_specs=[hbm] * 3 + [smem],
        out_shape=results,
        scratch_shapes=[
            pltpu.VMEM((2, KV_HEADS, devices) + tile, BF16),
            pltpu.VMEM((2, devices) + tile, F32),
            pltpu.VMEM((KV_HEADS, chips, 2) + tile, F32),
        ]
        + [per_head] * 6
        + [
            pltpu.VMEM((devices, 8, HEAD_DIM), F32),
            pltpu.VMEM((KV_HEADS, 8, HEAD_DIM), F32),
            pltpu.VMEM((devices, 8, HEAD_DIM), F32),
            pltpu.VMEM((dps, 8, HEAD_DIM), F32),
        ]
        + [pltpu.VMEM((here, HEADS * HEAD_DIM), BF16)] * 3
        + [pltpu.VMEM((here, flat), BF16)] * 2
        + [dma(step) for step in steps],
        compiler_params=pltpu.CompilerParams(
            collective_id=0, has_side_effects=True, vmem_limit_bytes=62 * 2**20
        ),
    )(queries[0], out_grad[0], key_states[0], value_states[0], sink_logit)
    query_grad, key_grad, value_grad, sink_grad = pl.pallas_call(
        place_kernel,
        in_specs=[hbm] * 3 + [smem],
        out_specs=[hbm] * 3 + [smem],
        out_shape=results,
        scratch_shapes=[pltpu.VMEM(result.shape, BF16) for result in results[:3]]
        + [dma((6,)), dma((6,))],
        compiler_params=pltpu.CompilerParams(vmem_limit_bytes=62 * 2**20),
    )(*held)
    return query_grad[None], key_grad[None], value_grad[None], sink_grad


def shards(queries, key_states, value_states, sink_logit, out_grad, block_table):
    devices = lax.axis_size("seq")
    dense = queries.shape[1] == BLOCK and devices == KB and devices == KV_HEADS
    part = dense_shards if dense else sparse_shards
    return part(queries, key_states, value_states, sink_logit, out_grad, block_table)


def solution(mesh):
    in_specs = (
        P("dp", "seq", None),
        P("dp", "seq", None),
        P("dp", "seq", None),
        P("seq"),
        P("dp", "seq", None),
        P("seq", None, None),
    )
    out_specs = (P("dp", "seq", None), P("dp", "seq", None), P("dp", "seq", None), P("seq"))
    return jax.shard_map(shards, mesh=mesh, in_specs=in_specs, out_specs=out_specs, check_vma=False)
```
